256 devices in a mesh: leaf: 64 (over z, x_lo, y), rhs: 4 (over x_hi, core).
Axes of the slice: x: 4 (x_hi: 2, x_lo: 2; x = x_hi * 2 + x_lo), y: 4, z: 8, core: 2. Of those that a mesh axis runs over, the one named last changes fastest.
Arguments:
- right_sides: bfloat16 [131072, 1536], P(('leaf', 'rhs')), may hold values from -6 to 6
- near_block: bfloat16 [131072, 2048], P('leaf'), may hold values from -0.125 to 0.125
- leaf_bases: bfloat16 [3, 131072, 128], P(None, 'leaf'), may hold values from -0.125 to 0.125
- couplings: float32 [3, 64, 128, 128], P(None, 'leaf'), may hold values from -0.5 to 0.5
- cluster_rows: int32 [64], P('leaf'), may hold values from 1 to 2048, 98304 in all
- nugget: float32 [131072], P(('leaf', 'rhs')), may hold values from 0.05 to 1
Outputs:
- product: bfloat16 [131072, 1536], P(('leaf', 'rhs'))
The draws below stay inside these ranges and needn't reach their ends.
Inputs may be any that keep to these rules, and one draw needn't show every extreme that they name: `cluster_rows`: the largest cluster fills its whole slot.
All inputs are finite; a program needn't handle non-finite values. No bound on the sum of `cluster_rows` on one device may be relied on, other than what follows from the above.
Results may differ from the reference program's by a relative error of at most 0.0051.
Values may be sent and summed in bfloat16 or wider, within the bound.
A program may use at most 64 MiB of HBM per device.

```python
import math
import jax
import jax.numpy as jnp
import numpy as np
from jax import lax

L = 2048
R = 128
LEVELS = 3
RHS = 1536
N = 131072
N_LEAF = 64


def level_of(stream_key, dims, cuts, least, top_value):
    def one(dim, shards_of):
        heights = jax.random.uniform(jax.random.fold_in(jax.random.fold_in(stream_key, 6), dim), (shards_of,), jnp.float32, least / len(cuts), top_value / len(cuts))
        return jnp.repeat(jnp.exp(heights), dims[dim] // shards_of).reshape((-1,) + (1,) * (len(dims) - dim - 1))

    gain = one(*cuts[0])
    for cut in cuts[1:]:
        gain = gain * one(*cut)
    return gain


def profile(amount, total, bound, skew):
    loads = [(1 << 20) // math.isqrt(rank ** skew) + 1 for rank in range(2, amount + 1)]
    spare, holding = total - bound - (amount - 1), [1] * (amount - 1)
    while spare > 0:
        movable = [i for i in range(amount - 1) if holding[i] < bound]
        pool, left = sum([loads[i] for i in movable]), spare
        for i in movable:
            more = min(bound - holding[i], max(1, left * loads[i] // pool), spare)
            holding[i] = holding[i] + more
            spare = spare - more
    return np.array([bound] + holding)


def ragged_sizes(stream_key, number_of, total, most, lean):
    if number_of == 2:
        one = jax.random.randint(stream_key, (), max(1, total - most), min(most, total - 1) + 1)
        return jnp.stack([one, total - one])
    lengths = jnp.asarray(profile(number_of, total, most, lean), jnp.int32)
    couples = (number_of - 1) // 2
    giver, sink = lengths[1:1 + 2 * couples:2], lengths[2:2 + 2 * couples:2]
    room = jnp.minimum(giver - 1, most - sink)
    passed = jax.random.randint(jax.random.fold_in(stream_key, 1), (couples,), 0, 1 << 20) % (room + 1)
    lengths = lengths.at[1:1 + 2 * couples:2].set(giver - passed).at[2:2 + 2 * couples:2].set(sink + passed)
    return lengths[jax.random.permutation(jax.random.fold_in(stream_key, 2), number_of)]


def noise(rng, shape, width, reach, shards=(), kind=jnp.bfloat16):
    factor_of = level_of(rng, shape, shards, -0.22, 0.18) if shards else 1.0
    array = jax.random.normal(rng, shape, jnp.float32) * width * factor_of
    return jnp.minimum(jnp.maximum(array, -reach), reach).astype(kind)


def setup_inputs(seed: int = 0) -> dict:
    seeds = jax.random.split(jax.random.key(seed), 7)
    return {
        "right_sides": noise(seeds[0], (N, RHS), 1.0, 6.0, ((0, 256),)),
        "near_block": noise(seeds[1], (N, L), L ** -0.5, 0.125, ((0, 64),)),
        "leaf_bases": noise(seeds[2], (LEVELS, N, R), L ** -0.5, 0.125, ((1, 64),)),
        "couplings": noise(seeds[3], (LEVELS, N_LEAF, R, R), R ** -0.5, 0.5, ((1, 64),), jnp.float32),
        "cluster_rows": ragged_sizes(seeds[4], N_LEAF, N_LEAF * L * 3 // 4, L, 0).astype(jnp.int32),
        "nugget": jnp.clip(jnp.exp(math.log(1.0) - 2.9957323 * jax.random.uniform(seeds[5], (N,), jnp.float32) ** level_of(seeds[5], (N,), ((0, 256),), -0.2, 0.2)), 0.05, 1.0),
    }


def leaf_dot(pair_args):
    return jnp.dot(pair_args[0], pair_args[1], preferred_element_type=jnp.float32)


def leaf_tdot(pair_args):
    return jnp.dot(pair_args[0].T, pair_args[1], preferred_element_type=jnp.float32)


def reference(right_sides, near_block, leaf_bases, couplings, cluster_rows, nugget):
    leaves = N_LEAF
    row_index = jnp.arange(L, dtype=jnp.int32)
    row_valid = row_index[None, :] < cluster_rows[:, None].astype(jnp.int32)
    blocks_x = right_sides.reshape(leaves, L, RHS)
    masked = jnp.where(row_valid[:, :, None], blocks_x, jnp.zeros_like(blocks_x))
    blocks_a = near_block.reshape(leaves, L, L)
    running = lax.map(leaf_dot, (blocks_a, masked))
    level_bases = leaf_bases.reshape(LEVELS, leaves, L, R)
    for tree_level in range(LEVELS):
        partial_sums = lax.map(leaf_tdot, (level_bases[tree_level], masked))
        span_size = 2 ** tree_level
        pairs = leaves // (2 * span_size)
        grouped = partial_sums.reshape(pairs, 2, span_size, R, RHS).sum(axis=2)
        sibling = grouped[:, ::-1]
        spread = jnp.broadcast_to(sibling[:, :, None], (pairs, 2, span_size, R, RHS)).reshape(leaves, R, RHS)
        mapped = jnp.einsum("nrs,nsc->nrc", couplings[tree_level], spread, precision=lax.Precision.HIGHEST).astype(jnp.bfloat16)
        running = running + lax.map(leaf_dot, (level_bases[tree_level], mapped))
    result_rows = jnp.where(row_valid[:, :, None], running, jnp.zeros_like(running)).astype(jnp.bfloat16)
    result_rows = lax.optimization_barrier(result_rows).reshape(leaves * L, RHS)
    masked_flat = masked.reshape(leaves * L, RHS)
    return (result_rows.astype(jnp.float32) + nugget[:, None] * masked_flat.astype(jnp.float32)).astype(jnp.bfloat16)
```

```python
import jax
import jax.numpy as jnp
from jax import lax
from jax.experimental import pallas as pl
from jax.experimental.pallas import tpu as pltpu
from jax.sharding import PartitionSpec as P

MESH = pl.DeviceIdType.MESH
BF16 = jnp.bfloat16
F32 = jnp.float32

LEAF = 2048
OWN = 512
PANEL = 384
PIECE = 128
PIECES = 3
RANK = 128
LEVELS = 3
PART = 32
BLOCK = 512


def kernel(
    x_hbm, near_hbm, bases_hbm, core_hbm, rows_smem, op_hbm,
    xs, relay, near, bases, bases_t, core, mask, total, result, back,
    out1, in1, sum2, out2, in2, sib2,
    local_sem, send_sem, recv_sem,
):
    leaf = lax.axis_index("leaf")
    rhs = lax.axis_index("rhs")
    y = leaf % 4
    x_lo = (leaf // 4) % 2
    panel = (rhs + 2 * x_lo) % 4
    mate = rhs + 1 - 2 * (rhs % 2)
    far = (rhs + 2) % 4
    mate_panel = panel + 1 - 2 * (panel % 2)
    far_panel = (panel + 2) % 4
    cross_panel = 3 - panel
    ys = (y + 1 - 2 * (y % 2), (y + 2) % 4, 3 - y)
    to_mate = (leaf, mate)
    to_far = (leaf, far)
    to_ys = tuple((leaf - y + other, rhs) for other in ys)
    to_pair = (leaf + 4 - 8 * x_lo, far)

    barrier = pltpu.get_barrier_semaphore()
    for device in (to_mate, to_far, *to_ys, to_pair):
        pl.semaphore_signal(barrier, inc=1, device_id=device, device_id_type=MESH)

    def rows_of(index):
        return pl.ds(pl.multiple_of(index * OWN, OWN), OWN)

    def cols_of(which, k):
        return pl.ds(pl.multiple_of(which * PANEL + k * PIECE, PIECE), PIECE)

    local = []

    def load(src, dst):
        copy = pltpu.make_async_copy(src, dst, local_sem.at[len(local)])
        copy.start()
        local.append(copy)
        return copy

    own_x = [load(x_hbm.at[:, cols_of(panel, k)], xs.at[k, rows_of(rhs)]) for k in range(PIECES)]
    load_bases = [
        load(bases_hbm.at[l], bases.at[:, pl.ds(l * RANK, RANK)]) for l in range(LEVELS)
    ]
    load_core = load(core_hbm, core)
    load_near = load(near_hbm, near)

    def remote(index, src, dst, device):
        return pltpu.make_async_remote_copy(
            src_ref=src, dst_ref=dst, send_sem=send_sem.at[index], recv_sem=recv_sem.at[index],
            device_id=device, device_id_type=MESH,
        )

    def copies(k):
        base = 15 * k
        c = {}
        c["relay"] = remote(base, x_hbm.at[:, cols_of(cross_panel, k)], relay.at[k], to_mate)
        c["mate"] = remote(
            base + 1, x_hbm.at[:, cols_of(mate_panel, k)], xs.at[k, rows_of(rhs)], to_mate
        )
        c["far"] = remote(
            base + 2, x_hbm.at[:, cols_of(far_panel, k)], xs.at[k, rows_of(rhs)], to_far
        )
        c["on"] = remote(base + 3, relay.at[k], xs.at[k, rows_of(mate)], to_far)
        c["one"] = [
            remote(base + 4 + j, out1.at[k, j], in1.at[k, j], to_ys[j]) for j in range(3)
        ]
        c["two"] = remote(base + 7, out2.at[k], in2.at[k], to_pair)
        mine = sib2.at[k, pl.ds(pl.multiple_of(y * PART, PART), PART)]
        c["three"] = [remote(base + 8 + j, in2.at[k], mine, to_ys[j]) for j in range(3)]
        c["back"] = remote(base + 11, result.at[k, rows_of(3 - rhs)], back.at[k], to_mate)
        c["rmate"] = remote(
            base + 12, result.at[k, rows_of(mate)], op_hbm.at[:, cols_of(panel, k)], to_mate
        )
        c["rfar"] = remote(
            base + 13, result.at[k, rows_of(far)], op_hbm.at[:, cols_of(panel, k)], to_far
        )
        c["ron"] = remote(
            base + 14, back.at[k], op_hbm.at[:, cols_of(mate_panel, k)], to_far
        )
        c["rown"] = pltpu.make_async_copy(
            result.at[k, rows_of(rhs)], op_hbm.at[:, cols_of(panel, k)], local_sem.at[8 + k]
        )
        return c

    every = [copies(k) for k in range(PIECES)]

    pl.semaphore_wait(barrier, 6)

    every[0]["relay"].start()
    every[0]["far"].start()
    every[1]["relay"].start()
    every[0]["mate"].start()
    every[2]["relay"].start()
    every[1]["mate"].start()
    every[2]["mate"].start()
    for k in range(PIECES):
        every[k]["relay"].wait_recv()
        every[k]["on"].start()
        if k + 1 < PIECES:
            every[k + 1]["far"].start()

    count = rows_smem[0]

    def make_mask(i, carry):
        at = pl.ds(pl.multiple_of(i * BLOCK, BLOCK), BLOCK)
        row = lax.broadcasted_iota(jnp.int32, (BLOCK, PIECE), 0) + i * BLOCK
        mask[at, :] = jnp.where(row < count, 1.0, 0.0).astype(BF16)
        return carry

    lax.fori_loop(0, LEAF // BLOCK, make_mask, 0)

    for copy in load_bases:
        copy.wait()
    for i in range(LEAF // BLOCK):
        at = pl.ds(i * BLOCK, BLOCK)
        bases_t[:, at] = bases[at, :].T

    def gather(k):
        c = every[k]
        own_x[k].wait()
        c["mate"].wait_recv()
        c["far"].wait_recv()
        c["on"].wait_recv()
        xs[k] = xs[k] * mask[...]
        part = jnp.dot(bases_t[...], xs[k], preferred_element_type=F32)
        sum2[k] = part[2 * RANK :]
        out1[k, 0, :RANK] = part[:RANK].astype(BF16)
        middle = part[RANK : 2 * RANK].astype(BF16)
        out1[k, 1, :RANK] = middle
        out1[k, 2, :RANK] = middle
        for j in range(3):
            at = pl.ds(pl.multiple_of(ys[j] * PART, PART), PART)
            out1[k, j, RANK:] = sum2[k, at].astype(BF16)
            c["one"][j].start()

    def near_field(k):
        def step(i, carry):
            at = pl.ds(pl.multiple_of(i * BLOCK, BLOCK), BLOCK)
            total[at, :] = jnp.dot(near[at, :], xs[k], preferred_element_type=F32)
            return carry

        lax.fori_loop(0, LEAF // BLOCK, step, 0)

    def exchange(k):
        c = every[k]
        for copy in c["one"]:
            copy.wait_recv()
        at = pl.ds(pl.multiple_of(y * PART, PART), PART)
        part = sum2[k, at]
        for j in range(3):
            part = part + in1[k, j, RANK:].astype(F32)
        out2[k] = part
        c["two"].start()

    def spread(k):
        c = every[k]
        c["two"].wait_recv()
        for copy in c["three"]:
            copy.start()

    def finish(k):
        c = every[k]
        at = pl.ds(pl.multiple_of(y * PART, PART), PART)
        sib2[k, at] = in2[k]
        for copy in c["three"]:
            copy.wait_recv()
        sibling = (
            in1[k, 0, :RANK].astype(F32),
            in1[k, 1, :RANK].astype(F32) + in1[k, 2, :RANK].astype(F32),
            sib2[k],
        )
        mapped = jnp.concatenate(
            [
                jnp.dot(
                    core[l, 0], sibling[l], precision=lax.Precision.HIGHEST,
                    preferred_element_type=F32,
                ).astype(BF16)
                for l in range(LEVELS)
            ],
            axis=0,
        )

        def step(i, carry):
            at = pl.ds(pl.multiple_of(i * BLOCK, BLOCK), BLOCK)
            value = total[at, :] + jnp.dot(bases[at, :], mapped, preferred_element_type=F32)
            result[k, at, :] = (value * mask[at, :].astype(F32)).astype(BF16)
            return carry

        lax.fori_loop(0, LEAF // BLOCK, step, 0)
        c["back"].start()
        c["rfar"].start()
        c["rmate"].start()
        c["rown"].start()

    def relay_back(k):
        every[k]["back"].wait_recv()
        every[k]["ron"].start()

    gather(0)
    load_near.wait()
    load_core.wait()
    near_field(0)
    exchange(0)
    spread(0)
    gather(1)
    finish(0)
    near_field(1)
    relay_back(0)
    exchange(1)
    spread(1)
    gather(2)
    finish(1)
    near_field(2)
    relay_back(1)
    exchange(2)
    spread(2)
    finish(2)
    relay_back(2)

    for k in range(PIECES):
        c = every[k]
        c["rown"].wait()
        for name in ("relay", "mate", "far", "on", "two", "back", "rmate", "rfar", "ron"):
            c[name].wait_send()
        for copy in c["one"] + c["three"]:
            copy.wait_send()
        for name in ("rmate", "rfar", "ron"):
            c[name].wait_recv()


def operator(right_sides, near_block, leaf_bases, couplings, cluster_rows):
    hbm = pl.BlockSpec(memory_space=pltpu.HBM)
    dma = pltpu.SemaphoreType.DMA
    return pl.pallas_call(
        kernel,
        out_shape=jax.ShapeDtypeStruct(right_sides.shape, BF16),
        in_specs=[hbm, hbm, hbm, hbm, pl.BlockSpec(memory_space=pltpu.SMEM)],
        out_specs=hbm,
        scratch_shapes=[
            pltpu.VMEM((PIECES, LEAF, PIECE), BF16),
            pltpu.VMEM((PIECES, OWN, PIECE), BF16),
            pltpu.VMEM((LEAF, LEAF), BF16),
            pltpu.VMEM((LEAF, LEVELS * RANK), BF16),
            pltpu.VMEM((LEVELS * RANK, LEAF), BF16),
            pltpu.VMEM((LEVELS, 1, RANK, RANK), F32),
            pltpu.VMEM((LEAF, PIECE), BF16),
            pltpu.VMEM((LEAF, PIECE), F32),
            pltpu.VMEM((PIECES, LEAF, PIECE), BF16),
            pltpu.VMEM((PIECES, OWN, PIECE), BF16),
            pltpu.VMEM((PIECES, 3, RANK + PART, PIECE), BF16),
            pltpu.VMEM((PIECES, 3, RANK + PART, PIECE), BF16),
            pltpu.VMEM((PIECES, RANK, PIECE), F32),
            pltpu.VMEM((PIECES, PART, PIECE), F32),
            pltpu.VMEM((PIECES, PART, PIECE), F32),
            pltpu.VMEM((PIECES, RANK, PIECE), F32),
            dma((11,)),
            dma((15 * PIECES,)),
            dma((15 * PIECES,)),
        ],
        compiler_params=pltpu.CompilerParams(
            collective_id=0, has_side_effects=True, vmem_limit_bytes=48 << 20
        ),
        cost_estimate=pl.CostEstimate(
            flops=4 * 10**9, bytes_accessed=15 * 10**6, transcendentals=0
        ),
        name="operator",
    )(right_sides, near_block, leaf_bases, couplings, cluster_rows)


def on_device(right_sides, near_block, leaf_bases, couplings, cluster_rows, nugget):
    rows = operator(right_sides, near_block, leaf_bases, couplings, cluster_rows)
    row = lax.axis_index("rhs") * OWN + jnp.arange(OWN, dtype=jnp.int32)
    masked = jnp.where((row < cluster_rows[0])[:, None], right_sides, jnp.zeros_like(right_sides))
    return (rows.astype(F32) + nugget[:, None] * masked.astype(F32)).astype(BF16)


def solution(mesh):
    in_specs = (
        P(("leaf", "rhs"), None),
        P("leaf", None),
        P(None, "leaf", None),
        P(None, "leaf", None, None),
        P("leaf"),
        P(("leaf", "rhs")),
    )
    return jax.shard_map(
        on_device, mesh=mesh, in_specs=in_specs, out_specs=P(("leaf", "rhs"), None), check_vma=False
    )
```

```python
import jax
import jax.numpy as jnp
from jax import lax
from jax.experimental import pallas as pl
from jax.experimental.pallas import tpu as pltpu
from jax.sharding import PartitionSpec as P

MESH = pl.DeviceIdType.MESH
BF16 = jnp.bfloat16
F32 = jnp.float32

LEAF = 2048
CHIP = 1024
OWN = 512
PIECE = 128
SENT = 2
KEPT = 2
PIECES = SENT + KEPT
PANEL = SENT * PIECE
KEPT_AT = 4 * PANEL
RANK = 128
LEVELS = 3
PART = 32
BLOCK = 512
LAST = PIECES - 1
COPIES = 18


def kernel(
    x_hbm, near_hbm, bases_hbm, core_hbm, rows_hbm, op_hbm,
    xs, relay, xm, near, bases, bases_t, core, rows, mask, total, result, back,
    out0, in0, out1, in1, sum2, out2, in2, sib2, in3,
    local_sem, send_sem, recv_sem,
):
    leaf = lax.axis_index("leaf")
    rhs = lax.axis_index("rhs")
    y = leaf % 4
    x_lo = (leaf // 4) % 2
    mate = rhs + 1 - 2 * (rhs % 2)
    far = (rhs + 2) % 4
    cross = 3 - rhs
    ys = (y + 1 - 2 * (y % 2), (y + 2) % 4, 3 - y)
    to_mate = (leaf, mate)
    to_far = (leaf, far)
    to_ys = tuple((leaf - y + other, rhs) for other in ys)
    to_pair = (leaf + 4 - 8 * x_lo, rhs)

    barrier = pltpu.get_barrier_semaphore()
    for device in (to_far, to_pair, *to_ys, to_mate):
        pl.semaphore_signal(barrier, inc=1, device_id=device, device_id_type=MESH)

    def rows_of(index):
        return pl.ds(pl.multiple_of(index * OWN, OWN), OWN)

    def cols_of(which, k):
        if k < SENT:
            at = which * PANEL + k * PIECE
        else:
            at = KEPT_AT + (which % 2) * KEPT * PIECE + (k - SENT) * PIECE
        return pl.ds(pl.multiple_of(at, PIECE), PIECE)

    def part_of(index):
        return pl.ds(pl.multiple_of(index * PART, PART), PART)

    local = []

    def load(src, dst):
        copy = pltpu.make_async_copy(src, dst, local_sem.at[len(local)])
        copy.start()
        local.append(copy)
        return copy

    load_rows = load(rows_hbm, rows)
    load_bases = [
        load(bases_hbm.at[l], bases.at[:, pl.ds(l * RANK, RANK)]) for l in range(LEVELS)
    ]

    def remote(index, src, dst, device):
        return pltpu.make_async_remote_copy(
            src_ref=src, dst_ref=dst, send_sem=send_sem.at[index], recv_sem=recv_sem.at[index],
            device_id=device, device_id_type=MESH,
        )

    def copies(k):
        at = COPIES * k
        c = {}
        if k < SENT:
            c["relay"] = remote(at, x_hbm.at[:, cols_of(cross, k)], relay.at[k], to_mate)
            passed = relay.at[k]
        else:
            passed = xs.at[k, rows_of(mate)]
        c["mate"] = remote(at + 1, x_hbm.at[:, cols_of(mate, k)], xs.at[k, rows_of(rhs)], to_mate)
        c["far"] = remote(at + 2, x_hbm.at[:, cols_of(far, k)], xs.at[k, rows_of(rhs)], to_far)
        c["on"] = remote(at + 3, passed, xs.at[k, rows_of(mate)], to_far)
        c["zero"] = [remote(at + 4 + j, out0.at[k, j], in0.at[k, j], to_ys[j]) for j in range(3)]
        if k < LAST:
            first = pl.ds(0, PART)
            c["one"] = [
                remote(at + 7 + j, out1.at[k, j], in1.at[k, j], to_ys[j]) for j in range(3)
            ]
            c["two"] = remote(at + 10, out2.at[k, first], in2.at[k, first], to_pair)
            c["three"] = [
                remote(at + 11 + j, in2.at[k, first], sib2.at[k, part_of(y)], to_ys[j])
                for j in range(3)
            ]
        else:
            c["two"] = remote(at + 10, out2.at[k], in2.at[k], to_pair)
            c["three"] = [remote(at + 11 + j, in2.at[k], in3.at[j], to_ys[j]) for j in range(3)]
        mine = op_hbm.at[:, cols_of(rhs, k)]
        if k < SENT:
            c["rfar"] = remote(at + 14, result.at[k, rows_of(far)], mine, to_far)
            c["back"] = remote(at + 15, result.at[k, rows_of(cross)], back.at[k], to_mate)
            c["ron"] = remote(at + 17, back.at[k], op_hbm.at[:, cols_of(mate, k)], to_far)
        c["rmate"] = remote(at + 16, result.at[k, rows_of(mate)], mine, to_mate)
        c["rown"] = pltpu.make_async_copy(result.at[k, rows_of(rhs)], mine, local_sem.at[10 + k])
        return c

    every = [copies(k) for k in range(PIECES)]

    pl.semaphore_wait(barrier, 6)

    every[0]["far"].start()
    for k in range(SENT):
        every[k]["relay"].start()
    for k in range(PIECES):
        every[k]["mate"].start()
    own_x = [load(x_hbm.at[:, cols_of(rhs, k)], xs.at[k, rows_of(rhs)]) for k in range(PIECES)]
    load_near = load(near_hbm, near)
    load_core = load(core_hbm, core)
    for k in range(SENT):
        every[k]["relay"].wait_recv()
        if k:
            every[k]["far"].start()
        every[k]["on"].start()
    every[2]["far"].start()

    load_rows.wait()
    count = rows[0]

    def make_mask(i, carry):
        at = pl.ds(pl.multiple_of(i * BLOCK, BLOCK), BLOCK)
        row = lax.broadcasted_iota(jnp.int32, (BLOCK, PIECE), 0) + i * BLOCK
        mask[at, :] = jnp.where(row < count, 1.0, 0.0).astype(BF16)
        return carry

    lax.fori_loop(0, LEAF // BLOCK, make_mask, 0)

    for copy in load_bases:
        copy.wait()

    def transpose(i, carry):
        at = pl.ds(pl.multiple_of(i * PIECE, PIECE), PIECE)
        for l in range(LEVELS):
            level = pl.ds(l * RANK, RANK)
            bases_t[level, at] = (bases[at, level] * mask[at, :]).T
        return carry

    lax.fori_loop(0, LEAF // PIECE, transpose, 0)

    def gather(k):
        c = every[k]
        own_x[k].wait()
        if k < SENT:
            c["mate"].wait_recv()
        c["far"].wait_recv()
        c["on"].wait_recv()
        part = jnp.dot(bases_t[...], xs[k], preferred_element_type=F32)
        if k < LAST:
            sum2[k] = part[2 * RANK :]
            for j in range(3):
                out1[k, j] = sum2[k, part_of(ys[j])].astype(BF16)
                c["one"][j].start()
        else:
            out2[k] = part[2 * RANK :].astype(BF16)
            c["two"].start()
        middle = part[RANK : 2 * RANK].astype(BF16)
        out0[k, 0] = part[:RANK].astype(BF16)
        out0[k, 1] = middle
        out0[k, 2] = middle
        for copy in c["zero"]:
            copy.start()

    def near_field(k):
        xm[...] = xs[k] * mask[...]
        if k < SENT:
            for i in range(LEAF // CHIP):
                at = pl.ds(i * CHIP, CHIP)
                total[k, at] = jnp.dot(near[at, :], xm[...], preferred_element_type=F32)
        else:
            at = pl.ds(pl.multiple_of((rhs // 2) * CHIP, CHIP), CHIP)
            total[k, at] = jnp.dot(near[at, :], xm[...], preferred_element_type=F32)

    def exchange(k):
        c = every[k]
        part = sum2[k, part_of(y)]
        for j in range(3):
            c["one"][j].wait_recv()
            part = part + in1[k, j].astype(F32)
        out2[k, :PART] = part.astype(BF16)
        c["two"].start()

    def spread(k):
        c = every[k]
        c["two"].wait_recv()
        for copy in c["three"]:
            copy.start()
        if k < LAST:
            sib2[k, part_of(y)] = in2[k, :PART]

    def finish(k):
        c = every[k]
        for copy in c["zero"] + c["three"]:
            copy.wait_recv()
        if k < LAST:
            top = sib2[k].astype(F32)
        else:
            top = in2[k].astype(F32)
            for j in range(3):
                top = top + in3[j].astype(F32)
        sibling = (
            in0[k, 0].astype(F32),
            in0[k, 1].astype(F32) + in0[k, 2].astype(F32),
            top,
        )
        mapped = jnp.concatenate(
            [
                jnp.dot(
                    core[l, 0], sibling[l], precision=lax.Precision.HIGHEST,
                    preferred_element_type=F32,
                ).astype(BF16)
                for l in range(LEVELS)
            ],
            axis=0,
        )
        owners = ((mate, "rmate"), (rhs, "rown"))
        if k < SENT:
            owners = ((far, "rfar"), (cross, "back")) + owners
        for owner, name in owners:
            at = rows_of(owner)
            value = total[k, at] + jnp.dot(bases[at, :], mapped, preferred_element_type=F32)
            result[k, at, :] = value.astype(BF16)
            c[name].start()

    gather(0)
    load_near.wait()
    load_core.wait()
    near_field(0)
    exchange(0)
    every[2]["mate"].wait_recv()
    every[2]["on"].start()
    every[3]["far"].start()
    gather(1)
    near_field(1)
    spread(0)
    exchange(1)
    every[3]["mate"].wait_recv()
    every[3]["on"].start()
    gather(2)
    near_field(2)
    finish(0)
    spread(1)
    exchange(2)
    gather(3)
    every[0]["back"].wait_recv()
    every[0]["ron"].start()
    near_field(3)
    finish(1)
    spread(2)
    every[1]["back"].wait_recv()
    every[1]["ron"].start()
    spread(3)
    finish(2)
    finish(3)

    for k in range(PIECES):
        c = every[k]
        c["rown"].wait()
        for name in ("relay", "mate", "far", "on", "two", "rfar", "back", "rmate", "ron"):
            if name in c:
                c[name].wait_send()
        for copy in c["zero"] + c.get("one", []) + c["three"]:
            copy.wait_send()
        for name in ("rmate", "rfar", "ron"):
            if name in c:
                c[name].wait_recv()


def operator(right_sides, near_block, leaf_bases, couplings, cluster_rows):
    hbm = pl.BlockSpec(memory_space=pltpu.HBM)
    dma = pltpu.SemaphoreType.DMA
    return pl.pallas_call(
        kernel,
        out_shape=jax.ShapeDtypeStruct(right_sides.shape, BF16),
        in_specs=[hbm] * 5,
        out_specs=hbm,
        scratch_shapes=[
            pltpu.VMEM((PIECES, LEAF, PIECE), BF16),
            pltpu.VMEM((SENT, OWN, PIECE), BF16),
            pltpu.VMEM((LEAF, PIECE), BF16),
            pltpu.VMEM((LEAF, LEAF), BF16),
            pltpu.VMEM((LEAF, LEVELS * RANK), BF16),
            pltpu.VMEM((LEVELS * RANK, LEAF), BF16),
            pltpu.VMEM((LEVELS, 1, RANK, RANK), F32),
            pltpu.SMEM((1,), jnp.int32),
            pltpu.VMEM((LEAF, PIECE), BF16),
            pltpu.VMEM((PIECES, LEAF, PIECE), F32),
            pltpu.VMEM((PIECES, LEAF, PIECE), BF16),
            pltpu.VMEM((SENT, OWN, PIECE), BF16),
            pltpu.VMEM((PIECES, 3, RANK, PIECE), BF16),
            pltpu.VMEM((PIECES, 3, RANK, PIECE), BF16),
            pltpu.VMEM((LAST, 3, PART, PIECE), BF16),
            pltpu.VMEM((LAST, 3, PART, PIECE), BF16),
            pltpu.VMEM((LAST, RANK, PIECE), F32),
            pltpu.VMEM((PIECES, RANK, PIECE), BF16),
            pltpu.VMEM((PIECES, RANK, PIECE), BF16),
            pltpu.VMEM((LAST, RANK, PIECE), BF16),
            pltpu.VMEM((3, RANK, PIECE), BF16),
            dma((10 + PIECES,)),
            dma((COPIES * PIECES,)),
            dma((COPIES * PIECES,)),
        ],
        compiler_params=pltpu.CompilerParams(
            collective_id=0, has_side_effects=True, vmem_limit_bytes=60 << 20
        ),
        cost_estimate=pl.CostEstimate(
            flops=4 * 10**9, bytes_accessed=15 * 10**6, transcendentals=0
        ),
        name="operator",
    )(right_sides, near_block, leaf_bases, couplings, cluster_rows)


def on_device(right_sides, near_block, leaf_bases, couplings, cluster_rows, nugget):
    rows = operator(right_sides, near_block, leaf_bases, couplings, cluster_rows)
    row = lax.axis_index("rhs") * OWN + jnp.arange(OWN, dtype=jnp.int32)
    value = rows.astype(F32) + nugget[:, None] * right_sides.astype(F32)
    return jnp.where((row < cluster_rows[0])[:, None], value, 0.0).astype(BF16)


def solution(mesh):
    in_specs = (
        P(("leaf", "rhs"), None),
        P("leaf", None),
        P(None, "leaf", None),
        P(None, "leaf", None, None),
        P("leaf"),
        P(("leaf", "rhs")),
    )
    return jax.shard_map(
        on_device, mesh=mesh, in_specs=in_specs, out_specs=P(("leaf", "rhs"), None), check_vma=False
    )
```

```python
import jax
import jax.numpy as jnp
from jax import lax
from jax.experimental import pallas as pl
from jax.experimental.pallas import tpu as pltpu
from jax.sharding import PartitionSpec as P

MESH = pl.DeviceIdType.MESH
BF16 = jnp.bfloat16
F32 = jnp.float32

LEAF = 2048
CHIP = 1024
OWN = 512
PIECE = 128
SENT = 2
KEPT = 2
PIECES = SENT + KEPT
PANEL = SENT * PIECE
KEPT_AT = 4 * PANEL
RANK = 128
LEVELS = 3
RHS = 1536
PART = 32
BLOCK = 512
LAST = PIECES - 1
COPIES = 18


def kernel(
    x_hbm, near_hbm, bases_hbm, core_hbm, rows_hbm, nugget_hbm, out,
    own, noise, scale, live, xs, relay, xm, near, bases, bases_t, core, rows, mask, total, result, back,
    out0, in0, out1, in1, sum2, out2, in2, sib2, in3,
    local_sem, send_sem, recv_sem,
):
    leaf = lax.axis_index("leaf")
    rhs = lax.axis_index("rhs")
    y = leaf % 4
    x_lo = (leaf // 4) % 2
    mate = rhs + 1 - 2 * (rhs % 2)
    far = (rhs + 2) % 4
    cross = 3 - rhs
    ys = (y + 1 - 2 * (y % 2), (y + 2) % 4, 3 - y)
    to_mate = (leaf, mate)
    to_far = (leaf, far)
    to_ys = tuple((leaf - y + other, rhs) for other in ys)
    to_pair = (leaf + 4 - 8 * x_lo, rhs)

    barrier = pltpu.get_barrier_semaphore()
    for device in (to_far, to_pair, *to_ys, to_mate):
        pl.semaphore_signal(barrier, inc=1, device_id=device, device_id_type=MESH)

    def rows_of(index):
        return pl.ds(pl.multiple_of(index * OWN, OWN), OWN)

    def cols_of(which, k):
        if k < SENT:
            at = which * PANEL + k * PIECE
        else:
            at = KEPT_AT + (which % 2) * KEPT * PIECE + (k - SENT) * PIECE
        return pl.ds(pl.multiple_of(at, PIECE), PIECE)

    def part_of(index):
        return pl.ds(pl.multiple_of(index * PART, PART), PART)

    local = []

    def load(src, dst):
        copy = pltpu.make_async_copy(src, dst, local_sem.at[len(local)])
        copy.start()
        local.append(copy)
        return copy

    load_rows = load(rows_hbm, rows)
    load_noise = load(nugget_hbm, noise)
    load_bases = [
        load(bases_hbm.at[l], bases.at[:, pl.ds(l * RANK, RANK)]) for l in range(LEVELS)
    ]

    def remote(index, src, dst, device):
        return pltpu.make_async_remote_copy(
            src_ref=src, dst_ref=dst, send_sem=send_sem.at[index], recv_sem=recv_sem.at[index],
            device_id=device, device_id_type=MESH,
        )

    def copies(k):
        at = COPIES * k
        c = {}
        if k < SENT:
            c["relay"] = remote(at, x_hbm.at[:, cols_of(cross, k)], relay.at[k], to_mate)
            passed = relay.at[k]
        else:
            passed = xs.at[k, rows_of(mate)]
        c["mate"] = remote(at + 1, x_hbm.at[:, cols_of(mate, k)], xs.at[k, rows_of(rhs)], to_mate)
        c["far"] = remote(at + 2, x_hbm.at[:, cols_of(far, k)], xs.at[k, rows_of(rhs)], to_far)
        c["on"] = remote(at + 3, passed, xs.at[k, rows_of(mate)], to_far)
        c["zero"] = [remote(at + 4 + j, out0.at[k, j], in0.at[k, j], to_ys[j]) for j in range(3)]
        if k < LAST:
            first = pl.ds(0, PART)
            c["one"] = [
                remote(at + 7 + j, out1.at[k, j], in1.at[k, j], to_ys[j]) for j in range(3)
            ]
            c["two"] = remote(at + 10, out2.at[k, first], in2.at[k, first], to_pair)
            c["three"] = [
                remote(at + 11 + j, in2.at[k, first], sib2.at[k, part_of(y)], to_ys[j])
                for j in range(3)
            ]
        else:
            c["two"] = remote(at + 10, out2.at[k], in2.at[k], to_pair)
            c["three"] = [remote(at + 11 + j, in2.at[k], in3.at[j], to_ys[j]) for j in range(3)]
        mine = out.at[:, cols_of(rhs, k)]
        if k < SENT:
            c["rfar"] = remote(at + 14, result.at[k, rows_of(far)], mine, to_far)
            c["back"] = remote(at + 15, result.at[k, rows_of(cross)], back.at[k], to_mate)
            c["ron"] = remote(at + 17, back.at[k], out.at[:, cols_of(mate, k)], to_far)
        c["rmate"] = remote(at + 16, result.at[k, rows_of(mate)], mine, to_mate)
        return c

    every = [copies(k) for k in range(PIECES)]

    pl.semaphore_wait(barrier, 6)

    every[0]["far"].start()
    for k in range(SENT):
        every[k]["relay"].start()
    for k in range(PIECES):
        every[k]["mate"].start()
    own_x = [load(x_hbm.at[:, cols_of(rhs, k)], xs.at[k, rows_of(rhs)]) for k in range(PIECES)]
    load_near = load(near_hbm, near)
    load_core = load(core_hbm, core)
    load_own = load(x_hbm, own)
    for k in range(SENT):
        every[k]["relay"].wait_recv()
        if k:
            every[k]["far"].start()
        every[k]["on"].start()
    every[2]["far"].start()

    load_rows.wait()
    count = rows[0]

    def make_mask(i, carry):
        at = pl.ds(pl.multiple_of(i * BLOCK, BLOCK), BLOCK)
        row = lax.broadcasted_iota(jnp.int32, (BLOCK, PIECE), 0) + i * BLOCK
        mask[at, :] = jnp.where(row < count, 1.0, 0.0).astype(BF16)
        return carry

    lax.fori_loop(0, LEAF // BLOCK, make_mask, 0)

    for copy in load_bases:
        copy.wait()

    def transpose(i, carry):
        at = pl.ds(pl.multiple_of(i * PIECE, PIECE), PIECE)
        for l in range(LEVELS):
            level = pl.ds(l * RANK, RANK)
            bases_t[level, at] = (bases[at, level] * mask[at, :]).T
        return carry

    lax.fori_loop(0, LEAF // PIECE, transpose, 0)

    load_noise.wait()
    for i in range(OWN // PIECE):
        at = pl.ds(i * PIECE, PIECE)
        spread_out = jnp.broadcast_to(noise[at].reshape(1, PIECE), (PIECE, PIECE)).T
        alive = mask[pl.ds(pl.multiple_of(rhs * OWN + i * PIECE, PIECE), PIECE), :].astype(F32)
        live[at, :] = alive
        scale[at, :] = spread_out * alive

    def add_noise(cols, value):
        out[:, cols] = (
            value.astype(F32) * live[...] + scale[...] * own[:, cols].astype(F32)
        ).astype(BF16)

    def settle(k, name, which):
        every[k][name].wait_recv()
        cols = cols_of(which, k)
        add_noise(cols, out[:, cols])

    def gather(k):
        c = every[k]
        own_x[k].wait()
        if k < SENT:
            c["mate"].wait_recv()
        c["far"].wait_recv()
        c["on"].wait_recv()
        part = jnp.dot(bases_t[...], xs[k], preferred_element_type=F32)
        if k < LAST:
            sum2[k] = part[2 * RANK :]
            for j in range(3):
                out1[k, j] = sum2[k, part_of(ys[j])].astype(BF16)
                c["one"][j].start()
        else:
            out2[k] = part[2 * RANK :].astype(BF16)
            c["two"].start()
        middle = part[RANK : 2 * RANK].astype(BF16)
        out0[k, 0] = part[:RANK].astype(BF16)
        out0[k, 1] = middle
        out0[k, 2] = middle
        for copy in c["zero"]:
            copy.start()

    def near_field(k):
        xm[...] = xs[k] * mask[...]
        if k < SENT:
            for i in range(LEAF // CHIP):
                at = pl.ds(i * CHIP, CHIP)
                total[k, at] = jnp.dot(near[at, :], xm[...], preferred_element_type=F32)
        else:
            at = pl.ds(pl.multiple_of((rhs // 2) * CHIP, CHIP), CHIP)
            total[k, at] = jnp.dot(near[at, :], xm[...], preferred_element_type=F32)

    def exchange(k):
        c = every[k]
        part = sum2[k, part_of(y)]
        for j in range(3):
            c["one"][j].wait_recv()
            part = part + in1[k, j].astype(F32)
        out2[k, :PART] = part.astype(BF16)
        c["two"].start()

    def spread(k):
        c = every[k]
        c["two"].wait_recv()
        for copy in c["three"]:
            copy.start()
        if k < LAST:
            sib2[k, part_of(y)] = in2[k, :PART]

    def finish(k):
        c = every[k]
        for copy in c["zero"] + c["three"]:
            copy.wait_recv()
        if k < LAST:
            top = sib2[k].astype(F32)
        else:
            top = in2[k].astype(F32)
            for j in range(3):
                top = top + in3[j].astype(F32)
        sibling = (
            in0[k, 0].astype(F32),
            in0[k, 1].astype(F32) + in0[k, 2].astype(F32),
            top,
        )
        mapped = jnp.concatenate(
            [
                jnp.dot(
                    core[l, 0], sibling[l], precision=lax.Precision.HIGHEST,
                    preferred_element_type=F32,
                ).astype(BF16)
                for l in range(LEVELS)
            ],
            axis=0,
        )
        owners = ((mate, "rmate"),)
        if k < SENT:
            owners = ((far, "rfar"), (cross, "back")) + owners
        for owner, name in owners:
            at = rows_of(owner)
            value = total[k, at] + jnp.dot(bases[at, :], mapped, preferred_element_type=F32)
            result[k, at, :] = value.astype(BF16)
            c[name].start()
        at = rows_of(rhs)
        value = total[k, at] + jnp.dot(bases[at, :], mapped, preferred_element_type=F32)
        add_noise(cols_of(rhs, k), value.astype(BF16))

    gather(0)
    load_near.wait()
    load_core.wait()
    load_own.wait()
    near_field(0)
    exchange(0)
    every[2]["mate"].wait_recv()
    every[2]["on"].start()
    every[3]["far"].start()
    gather(1)
    near_field(1)
    spread(0)
    exchange(1)
    every[3]["mate"].wait_recv()
    every[3]["on"].start()
    gather(2)
    near_field(2)
    finish(0)
    spread(1)
    exchange(2)
    gather(3)
    every[0]["back"].wait_recv()
    every[0]["ron"].start()
    near_field(3)
    finish(1)
    spread(2)
    every[1]["back"].wait_recv()
    every[1]["ron"].start()
    settle(0, "rmate", mate)
    settle(1, "rmate", mate)
    spread(3)
    settle(0, "rfar", far)
    finish(2)
    settle(0, "ron", cross)
    finish(3)
    settle(2, "rmate", mate)
    settle(1, "rfar", far)
    settle(3, "rmate", mate)
    settle(1, "ron", cross)

    for k in range(PIECES):
        c = every[k]
        for name in ("relay", "mate", "far", "on", "two", "rfar", "back", "rmate", "ron"):
            if name in c:
                c[name].wait_send()
        for copy in c["zero"] + c.get("one", []) + c["three"]:
            copy.wait_send()


def on_device(*arrays):
    hbm = pl.BlockSpec(memory_space=pltpu.HBM)
    dma = pltpu.SemaphoreType.DMA
    return pl.pallas_call(
        kernel,
        out_shape=pltpu.VMEM((OWN, RHS), BF16),
        in_specs=[hbm] * 6,
        out_specs=pl.BlockSpec(memory_space=pltpu.VMEM),
        scratch_shapes=[
            pltpu.VMEM((OWN, RHS), BF16),
            pltpu.VMEM((OWN,), F32),
            pltpu.VMEM((OWN, PIECE), F32),
            pltpu.VMEM((OWN, PIECE), F32),
            pltpu.VMEM((PIECES, LEAF, PIECE), BF16),
            pltpu.VMEM((SENT, OWN, PIECE), BF16),
            pltpu.VMEM((LEAF, PIECE), BF16),
            pltpu.VMEM((LEAF, LEAF), BF16),
            pltpu.VMEM((LEAF, LEVELS * RANK), BF16),
            pltpu.VMEM((LEVELS * RANK, LEAF), BF16),
            pltpu.VMEM((LEVELS, 1, RANK, RANK), F32),
            pltpu.SMEM((1,), jnp.int32),
            pltpu.VMEM((LEAF, PIECE), BF16),
            pltpu.VMEM((PIECES, LEAF, PIECE), F32),
            pltpu.VMEM((PIECES, LEAF, PIECE), BF16),
            pltpu.VMEM((SENT, OWN, PIECE), BF16),
            pltpu.VMEM((PIECES, 3, RANK, PIECE), BF16),
            pltpu.VMEM((PIECES, 3, RANK, PIECE), BF16),
            pltpu.VMEM((LAST, 3, PART, PIECE), BF16),
            pltpu.VMEM((LAST, 3, PART, PIECE), BF16),
            pltpu.VMEM((LAST, RANK, PIECE), F32),
            pltpu.VMEM((PIECES, RANK, PIECE), BF16),
            pltpu.VMEM((PIECES, RANK, PIECE), BF16),
            pltpu.VMEM((LAST, RANK, PIECE), BF16),
            pltpu.VMEM((3, RANK, PIECE), BF16),
            dma((12,)),
            dma((COPIES * PIECES,)),
            dma((COPIES * PIECES,)),
        ],
        compiler_params=pltpu.CompilerParams(
            collective_id=0, has_side_effects=True, vmem_limit_bytes=48 << 20
        ),
        cost_estimate=pl.CostEstimate(
            flops=4 * 10**9, bytes_accessed=15 * 10**6, transcendentals=0
        ),
        name="operator",
    )(
        *(pltpu.with_memory_space_constraint(array, pltpu.HBM) for array in arrays[:4]),
        arrays[4],
        pltpu.with_memory_space_constraint(arrays[5], pltpu.HBM),
    )


def solution(mesh):
    in_specs = (
        P(("leaf", "rhs"), None),
        P("leaf", None),
        P(None, "leaf", None),
        P(None, "leaf", None, None),
        P("leaf"),
        P(("leaf", "rhs")),
    )
    return jax.shard_map(
        on_device, mesh=mesh, in_specs=in_specs, out_specs=P(("leaf", "rhs"), None), check_vma=False
    )
```

```python
import jax
import jax.numpy as jnp
from jax import lax
from jax.experimental import pallas as pl
from jax.experimental.pallas import tpu as pltpu
from jax.sharding import PartitionSpec as P

MESH = pl.DeviceIdType.MESH
BF16 = jnp.bfloat16
F32 = jnp.float32

LEAF = 2048
CHIP = 1024
OWN = 512
PIECE = 128
SENT = 2
KEPT = 2
PIECES = SENT + KEPT
PANEL = SENT * PIECE
KEPT_AT = 4 * PANEL
RANK = 128
LEVELS = 3
RHS = 1536
PART = 32
BLOCK = 512
CROSS = (3,)
COPIES = 18


def kernel(
    x_hbm, near_hbm, bases_hbm, core_hbm, rows, nugget_hbm, out,
    own, noise, scale, live, xs, relay, xm, near, bases, bases_t, core, mask, total, total_kept, result, back,
    out0, in0, out1, in1, sum2, out2, in2, sib2, in3,
    local_sem, send_sem, recv_sem,
):
    leaf = lax.axis_index("leaf")
    rhs = lax.axis_index("rhs")
    y = leaf % 4
    x_lo = (leaf // 4) % 2
    mate = rhs + 1 - 2 * (rhs % 2)
    far = (rhs + 2) % 4
    cross = 3 - rhs
    ys = (y + 1 - 2 * (y % 2), (y + 2) % 4, 3 - y)
    to_mate = (leaf, mate)
    to_far = (leaf, far)
    to_ys = tuple((leaf - y + other, rhs) for other in ys)
    to_pair = (leaf + 4 - 8 * x_lo, rhs)

    barrier = pltpu.get_barrier_semaphore()
    for device in (to_far, to_pair, *to_ys, to_mate):
        pl.semaphore_signal(barrier, inc=1, device_id=device, device_id_type=MESH)

    def rows_of(index):
        return pl.ds(pl.multiple_of(index * OWN, OWN), OWN)

    def cols_of(which, k):
        if k < SENT:
            at = which * PANEL + k * PIECE
        else:
            at = KEPT_AT + (which % 2) * KEPT * PIECE + (k - SENT) * PIECE
        return pl.ds(pl.multiple_of(at, PIECE), PIECE)

    def part_of(index):
        return pl.ds(pl.multiple_of(index * PART, PART), PART)

    local = []

    def load(src, dst):
        copy = pltpu.make_async_copy(src, dst, local_sem.at[len(local)])
        copy.start()
        local.append(copy)
        return copy

    load_noise = load(nugget_hbm, noise)
    load_bases = [
        load(bases_hbm.at[l], bases.at[:, pl.ds(l * RANK, RANK)]) for l in range(LEVELS)
    ]

    def remote(index, src, dst, device):
        return pltpu.make_async_remote_copy(
            src_ref=src, dst_ref=dst, send_sem=send_sem.at[index], recv_sem=recv_sem.at[index],
            device_id=device, device_id_type=MESH,
        )

    def copies(k):
        at = COPIES * k
        c = {}
        if k < SENT:
            c["relay"] = remote(at, x_hbm.at[:, cols_of(cross, k)], relay.at[k], to_mate)
            passed = relay.at[k]
        else:
            passed = xs.at[k, rows_of(mate)]
        c["mate"] = remote(at + 1, x_hbm.at[:, cols_of(mate, k)], xs.at[k, rows_of(rhs)], to_mate)
        c["far"] = remote(at + 2, x_hbm.at[:, cols_of(far, k)], xs.at[k, rows_of(rhs)], to_far)
        c["on"] = remote(at + 3, passed, xs.at[k, rows_of(mate)], to_far)
        c["zero"] = [remote(at + 4 + j, out0.at[k, j], in0.at[k, j], to_ys[j]) for j in range(3)]
        if k not in CROSS:
            first = pl.ds(0, PART)
            c["one"] = [
                remote(at + 7 + j, out1.at[k, j], in1.at[k, j], to_ys[j]) for j in range(3)
            ]
            c["two"] = remote(at + 10, out2.at[k, first], in2.at[k, first], to_pair)
            c["three"] = [
                remote(at + 11 + j, in2.at[k, first], sib2.at[k, part_of(y)], to_ys[j])
                for j in range(3)
            ]
        else:
            c["two"] = remote(at + 10, out2.at[k], in2.at[k], to_pair)
            c["three"] = [remote(at + 11 + j, in2.at[k], in3.at[k, j], to_ys[j]) for j in range(3)]
        mine = out.at[:, cols_of(rhs, k)]
        if k < SENT:
            c["rfar"] = remote(at + 14, result.at[k, rows_of(far)], mine, to_far)
            c["back"] = remote(at + 15, result.at[k, rows_of(cross)], back.at[k], to_mate)
            c["ron"] = remote(at + 17, back.at[k], out.at[:, cols_of(mate, k)], to_far)
        c["rmate"] = remote(at + 16, result.at[k, rows_of(mate)], mine, to_mate)
        return c

    every = [copies(k) for k in range(PIECES)]

    pl.semaphore_wait(barrier, 6)

    every[0]["relay"].start()
    every[0]["far"].start()
    every[1]["relay"].start()
    every[0]["mate"].start()
    every[0]["relay"].wait_recv()
    every[0]["on"].start()
    own_x = [load(x_hbm.at[:, cols_of(rhs, k)], xs.at[k, rows_of(rhs)]) for k in range(PIECES)]
    for k in range(1, PIECES):
        every[k]["mate"].start()

    count = rows[0:1, :]

    def make_mask(i, carry):
        at = pl.ds(pl.multiple_of(i * BLOCK, BLOCK), BLOCK)
        row = lax.broadcasted_iota(jnp.int32, (BLOCK, PIECE), 0) + i * BLOCK
        mask[at, :] = jnp.where(row < count, 1.0, 0.0).astype(BF16)
        return carry

    lax.fori_loop(0, LEAF // BLOCK, make_mask, 0)

    for copy in load_bases:
        copy.wait()

    def transpose(i, carry):
        at = pl.ds(pl.multiple_of(i * PIECE, PIECE), PIECE)
        for l in range(LEVELS):
            level = pl.ds(l * RANK, RANK)
            bases_t[level, at] = (bases[at, level] * mask[at, :]).T
        return carry

    lax.fori_loop(0, LEAF // PIECE, transpose, 0)

    every[1]["relay"].wait_recv()
    every[1]["far"].start()
    every[1]["on"].start()
    every[2]["far"].start()
    load_near = load(near_hbm, near)
    load_core = load(core_hbm, core)
    load_own = load(x_hbm, own)

    load_noise.wait()
    for i in range(OWN // PIECE):
        at = pl.ds(i * PIECE, PIECE)
        spread_out = jnp.broadcast_to(noise[at].reshape(1, PIECE), (PIECE, PIECE)).T
        alive = mask[pl.ds(pl.multiple_of(rhs * OWN + i * PIECE, PIECE), PIECE), :].astype(F32)
        live[at, :] = alive
        scale[at, :] = spread_out * alive

    def add_noise(cols, value):
        out[:, cols] = (
            value.astype(F32) * live[...] + scale[...] * own[:, cols].astype(F32)
        ).astype(BF16)

    def settle(k, name, which):
        every[k][name].wait_recv()
        cols = cols_of(which, k)
        add_noise(cols, out[:, cols])

    def gather(k):
        c = every[k]
        own_x[k].wait()
        if k < SENT:
            c["mate"].wait_recv()
        c["far"].wait_recv()
        c["on"].wait_recv()
        part = jnp.dot(bases_t[...], xs[k], preferred_element_type=F32)
        if k not in CROSS:
            sum2[k] = part[2 * RANK :]
            for j in range(3):
                out1[k, j] = sum2[k, part_of(ys[j])].astype(BF16)
                c["one"][j].start()
        else:
            out2[k] = part[2 * RANK :].astype(BF16)
            c["two"].start()
        middle = part[RANK : 2 * RANK].astype(BF16)
        out0[k, 0] = part[:RANK].astype(BF16)
        out0[k, 1] = middle
        out0[k, 2] = middle
        for copy in c["zero"]:
            copy.start()

    def near_sent(half):
        if half == 0:
            for k in range(SENT):
                xm[:, k * PIECE : (k + 1) * PIECE] = xs[k] * mask[...]
        at = pl.ds(half * CHIP, CHIP)
        total[at, :] = jnp.dot(near[at, :], xm[...], preferred_element_type=F32)

    def near_kept():
        for k in range(KEPT):
            xm[:, k * PIECE : (k + 1) * PIECE] = xs[SENT + k] * mask[...]
        at = pl.ds(pl.multiple_of((rhs // 2) * CHIP, CHIP), CHIP)
        total_kept[...] = jnp.dot(near[at, :], xm[...], preferred_element_type=F32)

    def near_of(k, owner):
        if k < SENT:
            return total[rows_of(owner), k * PIECE : (k + 1) * PIECE]
        at = (k - SENT) * PIECE
        return total_kept[rows_of(owner % 2), at : at + PIECE]

    def exchange(k):
        c = every[k]
        part = sum2[k, part_of(y)]
        for j in range(3):
            c["one"][j].wait_recv()
            part = part + in1[k, j].astype(F32)
        out2[k, :PART] = part.astype(BF16)
        c["two"].start()

    def spread(k):
        c = every[k]
        c["two"].wait_recv()
        for copy in c["three"]:
            copy.start()
        if k not in CROSS:
            sib2[k, part_of(y)] = in2[k, :PART]

    def finish(k):
        c = every[k]
        for copy in c["zero"] + c["three"]:
            copy.wait_recv()
        if k not in CROSS:
            top = sib2[k].astype(F32)
        else:
            top = in2[k].astype(F32)
            for j in range(3):
                top = top + in3[k, j].astype(F32)
        sibling = (
            in0[k, 0].astype(F32),
            in0[k, 1].astype(F32) + in0[k, 2].astype(F32),
            top,
        )
        mapped = jnp.concatenate(
            [
                jnp.dot(
                    core[l, 0], sibling[l], precision=lax.Precision.HIGHEST,
                    preferred_element_type=F32,
                ).astype(BF16)
                for l in range(LEVELS)
            ],
            axis=0,
        )
        owners = ((mate, "rmate"),)
        if k < SENT:
            owners = ((far, "rfar"), (cross, "back")) + owners
        for owner, name in owners:
            at = rows_of(owner)
            value = near_of(k, owner) + jnp.dot(
                bases[at, :], mapped, preferred_element_type=F32
            )
            result[k, at, :] = value.astype(BF16)
            c[name].start()
        at = rows_of(rhs)
        value = near_of(k, rhs) + jnp.dot(bases[at, :], mapped, preferred_element_type=F32)
        add_noise(cols_of(rhs, k), value.astype(BF16))

    gather(0)
    load_near.wait()
    load_core.wait()
    load_own.wait()
    exchange(0)
    every[2]["mate"].wait_recv()
    every[2]["on"].start()
    every[3]["far"].start()
    gather(1)
    spread(0)
    near_sent(0)
    near_sent(1)
    exchange(1)
    every[3]["mate"].wait_recv()
    every[3]["on"].start()
    gather(2)
    finish(0)
    spread(1)
    exchange(2)
    gather(3)
    every[0]["back"].wait_recv()
    every[0]["ron"].start()
    finish(1)
    spread(2)
    every[1]["back"].wait_recv()
    every[1]["ron"].start()
    spread(3)
    near_kept()
    settle(0, "rmate", mate)
    settle(1, "rmate", mate)
    settle(0, "rfar", far)
    finish(2)
    settle(0, "ron", cross)
    finish(3)
    settle(2, "rmate", mate)
    settle(1, "rfar", far)
    settle(3, "rmate", mate)
    settle(1, "ron", cross)

    for k in range(PIECES):
        c = every[k]
        for name in ("relay", "mate", "far", "on", "two", "rfar", "back", "rmate", "ron"):
            if name in c:
                c[name].wait_send()
        for copy in c["zero"] + c.get("one", []) + c["three"]:
            copy.wait_send()


def on_device(*arrays):
    hbm = pl.BlockSpec(memory_space=pltpu.HBM)
    dma = pltpu.SemaphoreType.DMA
    return pl.pallas_call(
        kernel,
        out_shape=pltpu.VMEM((OWN, RHS), BF16),
        in_specs=[hbm] * 4 + [pl.BlockSpec(memory_space=pltpu.VMEM), hbm],
        out_specs=pl.BlockSpec(memory_space=pltpu.VMEM),
        scratch_shapes=[
            pltpu.VMEM((OWN, RHS), BF16),
            pltpu.VMEM((OWN,), F32),
            pltpu.VMEM((OWN, PIECE), F32),
            pltpu.VMEM((OWN, PIECE), F32),
            pltpu.VMEM((PIECES, LEAF, PIECE), BF16),
            pltpu.VMEM((SENT, OWN, PIECE), BF16),
            pltpu.VMEM((LEAF, SENT * PIECE), BF16),
            pltpu.VMEM((LEAF, LEAF), BF16),
            pltpu.VMEM((LEAF, LEVELS * RANK), BF16),
            pltpu.VMEM((LEVELS * RANK, LEAF), BF16),
            pltpu.VMEM((LEVELS, 1, RANK, RANK), F32),
            pltpu.VMEM((LEAF, PIECE), BF16),
            pltpu.VMEM((LEAF, SENT * PIECE), F32),
            pltpu.VMEM((CHIP, KEPT * PIECE), F32),
            pltpu.VMEM((PIECES, LEAF, PIECE), BF16),
            pltpu.VMEM((SENT, OWN, PIECE), BF16),
            pltpu.VMEM((PIECES, 3, RANK, PIECE), BF16),
            pltpu.VMEM((PIECES, 3, RANK, PIECE), BF16),
            pltpu.VMEM((PIECES, 3, PART, PIECE), BF16),
            pltpu.VMEM((PIECES, 3, PART, PIECE), BF16),
            pltpu.VMEM((PIECES, RANK, PIECE), F32),
            pltpu.VMEM((PIECES, RANK, PIECE), BF16),
            pltpu.VMEM((PIECES, RANK, PIECE), BF16),
            pltpu.VMEM((PIECES, RANK, PIECE), BF16),
            pltpu.VMEM((PIECES, 3, RANK, PIECE), BF16),
            dma((12,)),
            dma((COPIES * PIECES,)),
            dma((COPIES * PIECES,)),
        ],
        compiler_params=pltpu.CompilerParams(
            collective_id=0, has_side_effects=True, vmem_limit_bytes=48 << 20
        ),
        cost_estimate=pl.CostEstimate(
            flops=4 * 10**9, bytes_accessed=15 * 10**6, transcendentals=0
        ),
        name="operator",
    )(
        *(pltpu.with_memory_space_constraint(array, pltpu.HBM) for array in arrays[:4]),
        jnp.broadcast_to(arrays[4], (8, PIECE)),
        pltpu.with_memory_space_constraint(arrays[5], pltpu.HBM),
    )


def solution(mesh):
    in_specs = (
        P(("leaf", "rhs"), None),
        P("leaf", None),
        P(None, "leaf", None),
        P(None, "leaf", None, None),
        P("leaf"),
        P(("leaf", "rhs")),
    )
    return jax.shard_map(
        on_device, mesh=mesh, in_specs=in_specs, out_specs=P(("leaf", "rhs"), None), check_vma=False
    )
```

```python
import jax
import jax.numpy as jnp
from jax import lax
from jax.experimental import pallas as pl
from jax.experimental.pallas import tpu as pltpu
from jax.sharding import PartitionSpec as P

MESH = pl.DeviceIdType.MESH
BF16 = jnp.bfloat16
F32 = jnp.float32

LEAF = 2048
CHIP = 1024
OWN = 512
PIECE = 128
SENT = 2
KEPT = 2
PIECES = SENT + KEPT
PANEL = SENT * PIECE
KEPT_AT = 4 * PANEL
RANK = 128
LEVELS = 3
RHS = 1536
PART = 32
BLOCK = 512
EARLY = PIECES - 1
COPIES = 18


def kernel(
    x_hbm, near_hbm, bases_hbm, core_hbm, rows, nugget_hbm, out,
    own, noise, scale, live, xs, relay, xm, near, bases, bases_t, core, mask, total, total_kept, result, back,
    out0, in0, out1, in1, sum2, out2, in2, sib2, mine_half, out_half, in_half,
    local_sem, send_sem, recv_sem, ready,
):
    leaf = lax.axis_index("leaf")
    rhs = lax.axis_index("rhs")
    y = leaf % 4
    x_lo = (leaf // 4) % 2
    mate = rhs + 1 - 2 * (rhs % 2)
    far = (rhs + 2) % 4
    cross = 3 - rhs
    ys = (y + 1 - 2 * (y % 2), (y + 2) % 4, 3 - y)
    to_mate = (leaf, mate)
    to_far = (leaf, far)
    to_ys = tuple((leaf - y + other, rhs) for other in ys)
    to_pair = (leaf + 4 - 8 * x_lo, rhs)

    barrier = pltpu.get_barrier_semaphore()
    for device in (to_far, to_mate):
        pl.semaphore_signal(barrier, inc=1, device_id=device, device_id_type=MESH)
    for j in range(3):

        @pl.when(ys[j] > y)
        def _():
            pl.semaphore_signal(barrier, inc=1, device_id=to_ys[j], device_id_type=MESH)

    @pl.when(x_lo == 0)
    def _():
        pl.semaphore_signal(barrier, inc=1, device_id=to_pair, device_id_type=MESH)

    def rows_of(index):
        return pl.ds(pl.multiple_of(index * OWN, OWN), OWN)

    def cols_of(which, k):
        if k < SENT:
            at = which * PANEL + k * PIECE
        else:
            at = KEPT_AT + (which % 2) * KEPT * PIECE + (k - SENT) * PIECE
        return pl.ds(pl.multiple_of(at, PIECE), PIECE)

    def part_of(index):
        return pl.ds(pl.multiple_of(index * PART, PART), PART)

    local = []

    def load(src, dst):
        copy = pltpu.make_async_copy(src, dst, local_sem.at[len(local)])
        copy.start()
        local.append(copy)
        return copy

    load_noise = load(nugget_hbm, noise)
    load_bases = [
        load(bases_hbm.at[l], bases.at[:, pl.ds(l * RANK, RANK)]) for l in range(LEVELS)
    ]

    def remote(index, src, dst, device):
        return pltpu.make_async_remote_copy(
            src_ref=src, dst_ref=dst, send_sem=send_sem.at[index], recv_sem=recv_sem.at[index],
            device_id=device, device_id_type=MESH,
        )

    def copies(k):
        at = COPIES * k
        c = {}
        if k < SENT:
            c["relay"] = remote(at, x_hbm.at[:, cols_of(cross, k)], relay.at[k], to_mate)
            passed = relay.at[k]
        else:
            passed = xs.at[k, rows_of(mate)]
        c["mate"] = remote(at + 1, x_hbm.at[:, cols_of(mate, k)], xs.at[k, rows_of(rhs)], to_mate)
        c["far"] = remote(at + 2, x_hbm.at[:, cols_of(far, k)], xs.at[k, rows_of(rhs)], to_far)
        c["on"] = remote(at + 3, passed, xs.at[k, rows_of(mate)], to_far)
        c["zero"] = [remote(at + 4 + j, out0.at[k, j], in0.at[k, j], to_ys[j]) for j in range(3)]
        c["one"] = [remote(at + 7 + j, out1.at[k, j], in1.at[k, j], to_ys[j]) for j in range(3)]
        c["two"] = remote(at + 10, out2.at[k], in2.at[k], to_pair)
        c["three"] = [
            remote(at + 11 + j, in2.at[k], sib2.at[k, part_of(y)], to_ys[j]) for j in range(3)
        ]
        if k == EARLY:
            c["half"] = remote(at + 14, out_half, in_half, to_far)
        mine = out.at[:, cols_of(rhs, k)]
        if k < SENT:
            c["rfar"] = remote(at + 14, result.at[k, rows_of(far)], mine, to_far)
            c["back"] = remote(at + 15, result.at[k, rows_of(cross)], back.at[k], to_mate)
            c["ron"] = remote(at + 17, back.at[k], out.at[:, cols_of(mate, k)], to_far)
        c["rmate"] = remote(at + 16, result.at[k, rows_of(mate)], mine, to_mate)
        return c

    every = [copies(k) for k in range(PIECES)]

    pl.semaphore_wait(barrier, 2 + y + x_lo)

    every[0]["relay"].start()
    every[0]["far"].start()
    every[1]["relay"].start()
    every[0]["mate"].start()
    every[0]["relay"].wait_recv()
    every[0]["on"].start()
    own_x = [load(x_hbm.at[:, cols_of(rhs, k)], xs.at[k, rows_of(rhs)]) for k in range(PIECES)]
    for k in range(1, PIECES):
        every[k]["mate"].start()
    for j in range(3):

        @pl.when(ys[j] < y)
        def _():
            pl.semaphore_signal(ready, inc=1, device_id=to_ys[j], device_id_type=MESH)

    @pl.when(x_lo == 1)
    def _():
        pl.semaphore_signal(ready, inc=1, device_id=to_pair, device_id_type=MESH)

    count = rows[0:1, :]

    def make_mask(i, carry):
        at = pl.ds(pl.multiple_of(i * BLOCK, BLOCK), BLOCK)
        row = lax.broadcasted_iota(jnp.int32, (BLOCK, PIECE), 0) + i * BLOCK
        mask[at, :] = jnp.where(row < count, 1.0, 0.0).astype(BF16)
        return carry

    lax.fori_loop(0, LEAF // BLOCK, make_mask, 0)

    for copy in load_bases:
        copy.wait()

    def transpose(i, carry):
        at = pl.ds(pl.multiple_of(i * PIECE, PIECE), PIECE)
        for l in range(LEVELS):
            level = pl.ds(l * RANK, RANK)
            bases_t[level, at] = (bases[at, level] * mask[at, :]).T
        return carry

    lax.fori_loop(0, LEAF // PIECE, transpose, 0)

    every[1]["relay"].wait_recv()
    every[1]["far"].start()
    every[1]["on"].start()
    every[2]["far"].start()
    load_near = load(near_hbm, near)
    load_core = load(core_hbm, core)
    load_own = load(x_hbm, own)

    load_noise.wait()
    for i in range(OWN // PIECE):
        at = pl.ds(i * PIECE, PIECE)
        spread_out = jnp.broadcast_to(noise[at].reshape(1, PIECE), (PIECE, PIECE)).T
        alive = mask[pl.ds(pl.multiple_of(rhs * OWN + i * PIECE, PIECE), PIECE), :].astype(F32)
        live[at, :] = alive
        scale[at, :] = spread_out * alive

    def add_noise(cols, value):
        out[:, cols] = (
            value.astype(F32) * live[...] + scale[...] * own[:, cols].astype(F32)
        ).astype(BF16)

    def settle(k, name, which):
        every[k][name].wait_recv()
        cols = cols_of(which, k)
        add_noise(cols, out[:, cols])

    def send_parts(k, part):
        sum2[k] = part
        for j in range(3):
            out1[k, j] = sum2[k, part_of(ys[j])].astype(BF16)
            every[k]["one"][j].start()

    def gather(k):
        c = every[k]
        if k != EARLY:
            own_x[k].wait()
        if k < SENT:
            c["mate"].wait_recv()
        c["far"].wait_recv()
        c["on"].wait_recv()
        if k == EARLY:
            part = jnp.dot(bases_t[: 2 * RANK], xs[k], preferred_element_type=F32)
        else:
            part = jnp.dot(bases_t[...], xs[k], preferred_element_type=F32)
            send_parts(k, part[2 * RANK :])
        middle = part[RANK : 2 * RANK].astype(BF16)
        out0[k, 0] = part[:RANK].astype(BF16)
        out0[k, 1] = middle
        out0[k, 2] = middle
        for copy in c["zero"]:
            copy.start()

    def near_sent(half):
        if half == 0:
            for k in range(SENT):
                xm[:, k * PIECE : (k + 1) * PIECE] = xs[k] * mask[...]
        at = pl.ds(half * CHIP, CHIP)
        total[at, :] = jnp.dot(near[at, :], xm[...], preferred_element_type=F32)

    def near_kept():
        for k in range(KEPT):
            xm[:, k * PIECE : (k + 1) * PIECE] = xs[SENT + k] * mask[...]
        at = pl.ds(pl.multiple_of((rhs // 2) * CHIP, CHIP), CHIP)
        total_kept[...] = jnp.dot(near[at, :], xm[...], preferred_element_type=F32)

    def near_of(k, owner):
        if k < SENT:
            return total[rows_of(owner), k * PIECE : (k + 1) * PIECE]
        at = (k - SENT) * PIECE
        return total_kept[rows_of(owner % 2), at : at + PIECE]

    def quarter(k):
        part = sum2[k, part_of(y)]
        for j in range(3):
            every[k]["one"][j].wait_recv()
            part = part + in1[k, j].astype(F32)
        return part

    def exchange(k):
        out2[k] = quarter(k).astype(BF16)
        every[k]["two"].start()

    def early_parts():
        own_x[EARLY].wait()
        every[EARLY]["mate"].wait_recv()
        at = pl.ds(pl.multiple_of((rhs // 2) * CHIP, CHIP), CHIP)
        send_parts(
            EARLY,
            jnp.dot(bases_t[2 * RANK :, at], xs[EARLY, at], preferred_element_type=F32),
        )

    def early_half():
        part = quarter(EARLY)
        mine_half[...] = part
        out_half[...] = part.astype(BF16)
        every[EARLY]["half"].start()

    def early_exchange():
        every[EARLY]["half"].wait_recv()
        out2[EARLY] = (mine_half[...] + in_half[...].astype(F32)).astype(BF16)
        every[EARLY]["two"].start()

    def spread(k):
        c = every[k]
        c["two"].wait_recv()
        for copy in c["three"]:
            copy.start()
        sib2[k, part_of(y)] = in2[k]

    def finish(k):
        c = every[k]
        for copy in c["zero"] + c["three"]:
            copy.wait_recv()
        sibling = (
            in0[k, 0].astype(F32),
            in0[k, 1].astype(F32) + in0[k, 2].astype(F32),
            sib2[k].astype(F32),
        )
        mapped = jnp.concatenate(
            [
                jnp.dot(
                    core[l, 0], sibling[l], precision=lax.Precision.HIGHEST,
                    preferred_element_type=F32,
                ).astype(BF16)
                for l in range(LEVELS)
            ],
            axis=0,
        )
        owners = ((mate, "rmate"),)
        if k < SENT:
            owners = ((far, "rfar"), (cross, "back")) + owners
        for owner, name in owners:
            at = rows_of(owner)
            value = near_of(k, owner) + jnp.dot(
                bases[at, :], mapped, preferred_element_type=F32
            )
            result[k, at, :] = value.astype(BF16)
            c[name].start()
        at = rows_of(rhs)
        value = near_of(k, rhs) + jnp.dot(bases[at, :], mapped, preferred_element_type=F32)
        add_noise(cols_of(rhs, k), value.astype(BF16))


    @pl.when(y + x_lo < 4)
    def _():
        pl.semaphore_wait(ready, 4 - y - x_lo)

    early_parts()
    gather(0)
    load_near.wait()
    load_core.wait()
    load_own.wait()
    early_half()
    exchange(0)
    every[2]["mate"].wait_recv()
    every[2]["on"].start()
    every[3]["far"].start()
    gather(1)
    spread(0)
    near_sent(0)
    near_sent(1)
    early_exchange()
    exchange(1)
    every[3]["on"].start()
    gather(2)
    finish(0)
    spread(1)
    exchange(2)
    every[0]["back"].wait_recv()
    every[0]["ron"].start()
    spread(3)
    gather(3)
    finish(1)
    spread(2)
    every[1]["back"].wait_recv()
    every[1]["ron"].start()
    near_kept()
    finish(3)
    settle(0, "rmate", mate)
    settle(1, "rmate", mate)
    settle(0, "rfar", far)
    finish(2)
    settle(0, "ron", cross)
    settle(3, "rmate", mate)
    settle(2, "rmate", mate)
    settle(1, "rfar", far)
    settle(1, "ron", cross)

    for k in range(PIECES):
        c = every[k]
        for name in ("relay", "mate", "far", "on", "half", "two", "rfar", "back", "rmate", "ron"):
            if name in c:
                c[name].wait_send()
        for copy in c["zero"] + c["one"] + c["three"]:
            copy.wait_send()


def on_device(*arrays):
    hbm = pl.BlockSpec(memory_space=pltpu.HBM)
    dma = pltpu.SemaphoreType.DMA
    return pl.pallas_call(
        kernel,
        out_shape=pltpu.VMEM((OWN, RHS), BF16),
        in_specs=[hbm] * 4 + [pl.BlockSpec(memory_space=pltpu.VMEM), hbm],
        out_specs=pl.BlockSpec(memory_space=pltpu.VMEM),
        scratch_shapes=[
            pltpu.VMEM((OWN, RHS), BF16),
            pltpu.VMEM((OWN,), F32),
            pltpu.VMEM((OWN, PIECE), F32),
            pltpu.VMEM((OWN, PIECE), F32),
            pltpu.VMEM((PIECES, LEAF, PIECE), BF16),
            pltpu.VMEM((SENT, OWN, PIECE), BF16),
            pltpu.VMEM((LEAF, SENT * PIECE), BF16),
            pltpu.VMEM((LEAF, LEAF), BF16),
            pltpu.VMEM((LEAF, LEVELS * RANK), BF16),
            pltpu.VMEM((LEVELS * RANK, LEAF), BF16),
            pltpu.VMEM((LEVELS, 1, RANK, RANK), F32),
            pltpu.VMEM((LEAF, PIECE), BF16),
            pltpu.VMEM((LEAF, SENT * PIECE), F32),
            pltpu.VMEM((CHIP, KEPT * PIECE), F32),
            pltpu.VMEM((PIECES, LEAF, PIECE), BF16),
            pltpu.VMEM((SENT, OWN, PIECE), BF16),
            pltpu.VMEM((PIECES, 3, RANK, PIECE), BF16),
            pltpu.VMEM((PIECES, 3, RANK, PIECE), BF16),
            pltpu.VMEM((PIECES, 3, PART, PIECE), BF16),
            pltpu.VMEM((PIECES, 3, PART, PIECE), BF16),
            pltpu.VMEM((PIECES, RANK, PIECE), F32),
            pltpu.VMEM((PIECES, PART, PIECE), BF16),
            pltpu.VMEM((PIECES, PART, PIECE), BF16),
            pltpu.VMEM((PIECES, RANK, PIECE), BF16),
            pltpu.VMEM((PART, PIECE), F32),
            pltpu.VMEM((PART, PIECE), BF16),
            pltpu.VMEM((PART, PIECE), BF16),
            dma((12,)),
            dma((COPIES * PIECES,)),
            dma((COPIES * PIECES,)),
            pltpu.SemaphoreType.REGULAR,
        ],
        compiler_params=pltpu.CompilerParams(
            collective_id=0, has_side_effects=True, vmem_limit_bytes=48 << 20
        ),
        cost_estimate=pl.CostEstimate(
            flops=4 * 10**9, bytes_accessed=15 * 10**6, transcendentals=0
        ),
        name="operator",
    )(
        *(pltpu.with_memory_space_constraint(array, pltpu.HBM) for array in arrays[:4]),
        jnp.broadcast_to(arrays[4], (8, PIECE)),
        pltpu.with_memory_space_constraint(arrays[5], pltpu.HBM),
    )


def solution(mesh):
    in_specs = (
        P(("leaf", "rhs"), None),
        P("leaf", None),
        P(None, "leaf", None),
        P(None, "leaf", None, None),
        P("leaf"),
        P(("leaf", "rhs")),
    )
    return jax.shard_map(
        on_device, mesh=mesh, in_specs=in_specs, out_specs=P(("leaf", "rhs"), None), check_vma=False
    )
```

```python
import jax
import jax.numpy as jnp
from jax import lax
from jax.experimental import pallas as pl
from jax.experimental.pallas import tpu as pltpu
from jax.sharding import PartitionSpec as P

MESH = pl.DeviceIdType.MESH
BF16 = jnp.bfloat16
F32 = jnp.float32

LEAF = 2048
CHIP = 1024
OWN = 512
PIECE = 128
SENT = 2
KEPT = 2
PIECES = SENT + KEPT
PANEL = SENT * PIECE
KEPT_AT = 4 * PANEL
RANK = 128
LEVELS = 3
RHS = 1536
PART = 32
BLOCK = 512
EARLY = PIECES - 1
COPIES = 18


def kernel(
    x_hbm, near_hbm, bases_hbm, core_hbm, rows, nugget_hbm, out,
    own, noise, scale, live, xs, relay, xm, near, bases, bases_t, core, mask,
    total, total_kept, result, back,
    out0, in0, out1, in1, sum2, out2, in2, sib2, mine_half, out_half, in_half,
    local_sem, send_sem, recv_sem, ready,
):
    leaf = lax.axis_index("leaf")
    rhs = lax.axis_index("rhs")
    y = leaf % 4
    x_lo = (leaf // 4) % 2
    mate = rhs + 1 - 2 * (rhs % 2)
    far = (rhs + 2) % 4
    cross = 3 - rhs
    ys = (y + 1 - 2 * (y % 2), (y + 2) % 4, 3 - y)
    to_mate = (leaf, mate)
    to_far = (leaf, far)
    to_ys = tuple((leaf - y + other, rhs) for other in ys)
    to_pair = (leaf + 4 - 8 * x_lo, rhs)

    barrier = pltpu.get_barrier_semaphore()
    for device in (to_far, to_mate):
        pl.semaphore_signal(barrier, inc=1, device_id=device, device_id_type=MESH)
    for j in range(3):

        @pl.when(ys[j] > y)
        def _():
            pl.semaphore_signal(barrier, inc=1, device_id=to_ys[j], device_id_type=MESH)

    @pl.when(x_lo == 0)
    def _():
        pl.semaphore_signal(barrier, inc=1, device_id=to_pair, device_id_type=MESH)

    def rows_of(index):
        return pl.ds(pl.multiple_of(index * OWN, OWN), OWN)

    def cols_of(which, k):
        if k < SENT:
            at = which * PANEL + k * PIECE
        else:
            at = KEPT_AT + (which % 2) * KEPT * PIECE + (k - SENT) * PIECE
        return pl.ds(pl.multiple_of(at, PIECE), PIECE)

    def part_of(index):
        return pl.ds(pl.multiple_of(index * PART, PART), PART)

    local = []

    def load(src, dst):
        copy = pltpu.make_async_copy(src, dst, local_sem.at[len(local)])
        copy.start()
        local.append(copy)
        return copy

    def remote(index, src, dst, device):
        return pltpu.make_async_remote_copy(
            src_ref=src, dst_ref=dst, send_sem=send_sem.at[index], recv_sem=recv_sem.at[index],
            device_id=device, device_id_type=MESH,
        )

    def copies(k):
        at = COPIES * k
        c = {}
        if k < SENT:
            c["relay"] = remote(at, x_hbm.at[:, cols_of(cross, k)], relay.at[k], to_mate)
            passed = relay.at[k]
        else:
            passed = xs.at[k, rows_of(mate)]
        c["mate"] = remote(at + 1, x_hbm.at[:, cols_of(mate, k)], xs.at[k, rows_of(rhs)], to_mate)
        c["far"] = remote(at + 2, x_hbm.at[:, cols_of(far, k)], xs.at[k, rows_of(rhs)], to_far)
        c["on"] = remote(at + 3, passed, xs.at[k, rows_of(mate)], to_far)
        c["zero"] = [remote(at + 4 + j, out0.at[k, j], in0.at[k, j], to_ys[j]) for j in range(3)]
        c["one"] = [remote(at + 7 + j, out1.at[k, j], in1.at[k, j], to_ys[j]) for j in range(3)]
        c["two"] = remote(at + 10, out2.at[k], in2.at[k], to_pair)
        c["three"] = [
            remote(at + 11 + j, in2.at[k], sib2.at[k, part_of(y)], to_ys[j]) for j in range(3)
        ]
        if k == EARLY:
            c["half"] = remote(at + 14, out_half, in_half, to_far)
        mine = out.at[:, cols_of(rhs, k)]
        if k < SENT:
            c["rfar"] = remote(at + 14, result.at[k, rows_of(far)], mine, to_far)
            c["back"] = remote(at + 15, result.at[k, rows_of(cross)], back.at[k], to_mate)
            c["ron"] = remote(at + 17, back.at[k], out.at[:, cols_of(mate, k)], to_far)
        c["rmate"] = remote(at + 16, result.at[k, rows_of(mate)], mine, to_mate)
        return c

    every = [copies(k) for k in range(PIECES)]

    pl.semaphore_wait(barrier, 2 + y + x_lo)

    every[0]["far"].start()
    every[0]["relay"].start()
    every[1]["relay"].start()
    every[0]["mate"].start()
    load_noise = load(nugget_hbm, noise)
    load_bases = [
        load(bases_hbm.at[l], bases.at[:, pl.ds(l * RANK, RANK)]) for l in range(LEVELS)
    ]
    every[0]["relay"].wait_recv()
    every[0]["on"].start()
    own_x = [load(x_hbm.at[:, cols_of(rhs, k)], xs.at[k, rows_of(rhs)]) for k in range(PIECES)]
    for k in range(1, PIECES):
        every[k]["mate"].start()
    for j in range(3):

        @pl.when(ys[j] < y)
        def _():
            pl.semaphore_signal(ready, inc=1, device_id=to_ys[j], device_id_type=MESH)

    @pl.when(x_lo == 1)
    def _():
        pl.semaphore_signal(ready, inc=1, device_id=to_pair, device_id_type=MESH)

    count = rows[0:1, :]

    def make_mask(i, carry):
        at = pl.ds(pl.multiple_of(i * BLOCK, BLOCK), BLOCK)
        row = lax.broadcasted_iota(jnp.int32, (BLOCK, PIECE), 0) + i * BLOCK
        mask[at, :] = jnp.where(row < count, 1.0, 0.0).astype(BF16)
        return carry

    lax.fori_loop(0, LEAF // BLOCK, make_mask, 0)

    for copy in load_bases:
        copy.wait()

    def transpose(i, carry):
        at = pl.ds(pl.multiple_of(i * PIECE, PIECE), PIECE)
        for l in range(LEVELS):
            level = pl.ds(l * RANK, RANK)
            bases_t[level, at] = (bases[at, level] * mask[at, :]).T
        return carry

    lax.fori_loop(0, LEAF // PIECE, transpose, 0)

    every[1]["relay"].wait_recv()
    every[1]["far"].start()
    every[1]["on"].start()
    every[2]["far"].start()
    load_near = load(near_hbm, near)
    load_core = load(core_hbm, core)
    load_own = load(x_hbm, own)

    load_noise.wait()
    for i in range(OWN // PIECE):
        at = pl.ds(i * PIECE, PIECE)
        spread_out = jnp.broadcast_to(noise[at].reshape(1, PIECE), (PIECE, PIECE)).T
        alive = mask[pl.ds(pl.multiple_of(rhs * OWN + i * PIECE, PIECE), PIECE), :].astype(F32)
        live[at, :] = alive
        scale[at, :] = spread_out * alive

    def add_noise(cols, value):
        out[:, cols] = (
            value.astype(F32) * live[...] + scale[...] * own[:, cols].astype(F32)
        ).astype(BF16)

    def settle(k, name, which):
        every[k][name].wait_recv()
        cols = cols_of(which, k)
        add_noise(cols, out[:, cols])

    def send_parts(k, part):
        sum2[k] = part
        for j in range(3):
            out1[k, j] = sum2[k, part_of(ys[j])].astype(BF16)
            every[k]["one"][j].start()

    def gather(k):
        c = every[k]
        if k != EARLY:
            own_x[k].wait()
        if k < SENT:
            c["mate"].wait_recv()
        c["far"].wait_recv()
        c["on"].wait_recv()
        if k == EARLY:
            part = jnp.dot(bases_t[: 2 * RANK], xs[k], preferred_element_type=F32)
        else:
            part = jnp.dot(bases_t[...], xs[k], preferred_element_type=F32)
            send_parts(k, part[2 * RANK :])
        middle = part[RANK : 2 * RANK].astype(BF16)
        out0[k, 0] = part[:RANK].astype(BF16)
        out0[k, 1] = middle
        out0[k, 2] = middle
        for copy in c["zero"]:
            copy.start()

    def near_sent(half):
        if half == 0:
            for k in range(SENT):
                xm[:, k * PIECE : (k + 1) * PIECE] = xs[k] * mask[...]
        at = pl.ds(half * CHIP, CHIP)
        total[at, :] = jnp.dot(near[at, :], xm[...], preferred_element_type=F32)

    def near_kept():
        for k in range(KEPT):
            xm[:, k * PIECE : (k + 1) * PIECE] = xs[SENT + k] * mask[...]
        at = pl.ds(pl.multiple_of((rhs // 2) * CHIP, CHIP), CHIP)
        total_kept[...] = jnp.dot(near[at, :], xm[...], preferred_element_type=F32)

    def near_of(k, owner):
        if k < SENT:
            return total[rows_of(owner), k * PIECE : (k + 1) * PIECE]
        at = (k - SENT) * PIECE
        return total_kept[rows_of(owner % 2), at : at + PIECE]

    def quarter(k):
        part = sum2[k, part_of(y)]
        for j in range(3):
            every[k]["one"][j].wait_recv()
            part = part + in1[k, j].astype(F32)
        return part

    def exchange(k):
        out2[k] = quarter(k).astype(BF16)
        every[k]["two"].start()

    def early_parts():
        own_x[EARLY].wait()
        every[EARLY]["mate"].wait_recv()
        at = pl.ds(pl.multiple_of((rhs // 2) * CHIP, CHIP), CHIP)
        send_parts(
            EARLY,
            jnp.dot(bases_t[2 * RANK :, at], xs[EARLY, at], preferred_element_type=F32),
        )

    def early_half():
        part = quarter(EARLY)
        mine_half[...] = part
        out_half[...] = part.astype(BF16)
        every[EARLY]["half"].start()

    def early_exchange():
        every[EARLY]["half"].wait_recv()
        out2[EARLY] = (mine_half[...] + in_half[...].astype(F32)).astype(BF16)
        every[EARLY]["two"].start()

    def spread(k):
        c = every[k]
        c["two"].wait_recv()
        for copy in c["three"]:
            copy.start()
        sib2[k, part_of(y)] = in2[k]

    def finish(k):
        c = every[k]
        for copy in c["zero"] + c["three"]:
            copy.wait_recv()
        sibling = (
            in0[k, 0].astype(F32),
            in0[k, 1].astype(F32) + in0[k, 2].astype(F32),
            sib2[k].astype(F32),
        )
        mapped = jnp.concatenate(
            [
                jnp.dot(
                    core[l, 0], sibling[l], precision=lax.Precision.HIGHEST,
                    preferred_element_type=F32,
                ).astype(BF16)
                for l in range(LEVELS)
            ],
            axis=0,
        )
        owners = ((mate, "rmate"),)
        if k < SENT:
            first = ((far, "rfar"), (cross, "back"))
            owners = (first[::-1] if k else first) + owners
        for owner, name in owners:
            at = rows_of(owner)
            value = near_of(k, owner) + jnp.dot(
                bases[at, :], mapped, preferred_element_type=F32
            )
            result[k, at, :] = value.astype(BF16)
            c[name].start()
        at = rows_of(rhs)
        value = near_of(k, rhs) + jnp.dot(bases[at, :], mapped, preferred_element_type=F32)
        add_noise(cols_of(rhs, k), value.astype(BF16))

    @pl.when(y + x_lo < 4)
    def _():
        pl.semaphore_wait(ready, 4 - y - x_lo)

    early_parts()
    gather(0)
    load_near.wait()
    load_core.wait()
    load_own.wait()
    early_half()
    exchange(0)
    every[2]["mate"].wait_recv()
    every[2]["on"].start()
    every[3]["far"].start()
    gather(1)
    spread(0)
    near_sent(0)
    near_sent(1)
    early_exchange()
    exchange(1)
    every[3]["on"].start()
    gather(2)
    finish(0)
    spread(1)
    exchange(2)
    every[0]["back"].wait_recv()
    every[0]["ron"].start()
    spread(3)
    gather(3)
    finish(1)
    every[1]["back"].wait_recv()
    every[1]["ron"].start()
    spread(2)
    near_kept()
    finish(3)
    settle(0, "rmate", mate)
    settle(1, "rmate", mate)
    settle(0, "rfar", far)
    finish(2)
    settle(0, "ron", cross)
    settle(3, "rmate", mate)
    settle(2, "rmate", mate)
    for k in range(PIECES):
        c = every[k]
        for name in ("relay", "mate", "far", "on", "half", "two", "rfar", "back", "rmate", "ron"):
            if name in c and c[name] is not every[1]["ron"]:
                c[name].wait_send()
        for copy in c["zero"] + c["one"] + c["three"]:
            copy.wait_send()
    settle(1, "rfar", far)
    settle(1, "ron", cross)
    every[1]["ron"].wait_send()


def on_device(*arrays):
    hbm = pl.BlockSpec(memory_space=pltpu.HBM)
    dma = pltpu.SemaphoreType.DMA
    return pl.pallas_call(
        kernel,
        out_shape=pltpu.VMEM((OWN, RHS), BF16),
        in_specs=[hbm] * 4 + [pl.BlockSpec(memory_space=pltpu.VMEM), hbm],
        out_specs=pl.BlockSpec(memory_space=pltpu.VMEM),
        scratch_shapes=[
            pltpu.VMEM((OWN, RHS), BF16),
            pltpu.VMEM((OWN,), F32),
            pltpu.VMEM((OWN, PIECE), F32),
            pltpu.VMEM((OWN, PIECE), F32),
            pltpu.VMEM((PIECES, LEAF, PIECE), BF16),
            pltpu.VMEM((SENT, OWN, PIECE), BF16),
            pltpu.VMEM((LEAF, SENT * PIECE), BF16),
            pltpu.VMEM((LEAF, LEAF), BF16),
            pltpu.VMEM((LEAF, LEVELS * RANK), BF16),
            pltpu.VMEM((LEVELS * RANK, LEAF), BF16),
            pltpu.VMEM((LEVELS, 1, RANK, RANK), F32),
            pltpu.VMEM((LEAF, PIECE), BF16),
            pltpu.VMEM((LEAF, SENT * PIECE), F32),
            pltpu.VMEM((CHIP, KEPT * PIECE), F32),
            pltpu.VMEM((PIECES, LEAF, PIECE), BF16),
            pltpu.VMEM((SENT, OWN, PIECE), BF16),
            pltpu.VMEM((PIECES, 3, RANK, PIECE), BF16),
            pltpu.VMEM((PIECES, 3, RANK, PIECE), BF16),
            pltpu.VMEM((PIECES, 3, PART, PIECE), BF16),
            pltpu.VMEM((PIECES, 3, PART, PIECE), BF16),
            pltpu.VMEM((PIECES, RANK, PIECE), F32),
            pltpu.VMEM((PIECES, PART, PIECE), BF16),
            pltpu.VMEM((PIECES, PART, PIECE), BF16),
            pltpu.VMEM((PIECES, RANK, PIECE), BF16),
            pltpu.VMEM((PART, PIECE), F32),
            pltpu.VMEM((PART, PIECE), BF16),
            pltpu.VMEM((PART, PIECE), BF16),
            dma((12,)),
            dma((COPIES * PIECES,)),
            dma((COPIES * PIECES,)),
            pltpu.SemaphoreType.REGULAR,
        ],
        compiler_params=pltpu.CompilerParams(
            collective_id=0, has_side_effects=True, vmem_limit_bytes=48 << 20
        ),
        cost_estimate=pl.CostEstimate(
            flops=4 * 10**9, bytes_accessed=15 * 10**6, transcendentals=0
        ),
        name="operator",
    )(
        *(pltpu.with_memory_space_constraint(array, pltpu.HBM) for array in arrays[:4]),
        jnp.broadcast_to(arrays[4], (8, PIECE)),
        pltpu.with_memory_space_constraint(arrays[5], pltpu.HBM),
    )


def solution(mesh):
    in_specs = (
        P(("leaf", "rhs"), None),
        P("leaf", None),
        P(None, "leaf", None),
        P(None, "leaf", None, None),
        P("leaf"),
        P(("leaf", "rhs")),
    )
    return jax.shard_map(
        on_device, mesh=mesh, in_specs=in_specs, out_specs=P(("leaf", "rhs"), None), check_vma=False
    )
```

```python
import jax
import jax.numpy as jnp
from jax import lax
from jax.experimental import pallas as pl
from jax.experimental.pallas import tpu as pltpu
from jax.sharding import PartitionSpec as P

MESH = pl.DeviceIdType.MESH
BF16 = jnp.bfloat16
F32 = jnp.float32

LEAF = 2048
CHIP = 1024
OWN = 512
PIECE = 128
SENT = 2
KEPT = 2
PIECES = SENT + KEPT
PANEL = SENT * PIECE
KEPT_AT = 4 * PANEL
RANK = 128
LEVELS = 3
RHS = 1536
PART = 32
BLOCK = 512
EARLY = PIECES - 1
COPIES = 18


def kernel(
    x_hbm, near_hbm, bases_hbm, core_hbm, rows, nugget_hbm, out,
    own, noise, scale, live, xs, relay, xm, near, bases, bases_t, core, mask,
    total, total_kept, result, back,
    out0, in0, out1, in1, sum2, out2, in2, sib2, mine_half, out_half, in_half,
    local_sem, send_sem, recv_sem, ready,
):
    leaf = lax.axis_index("leaf")
    rhs = lax.axis_index("rhs")
    y = leaf % 4
    x_lo = (leaf // 4) % 2
    mate = rhs + 1 - 2 * (rhs % 2)
    far = (rhs + 2) % 4
    cross = 3 - rhs
    ys = (y + 1 - 2 * (y % 2), (y + 2) % 4, 3 - y)
    to_mate = (leaf, mate)
    to_far = (leaf, far)
    to_ys = tuple((leaf - y + other, rhs) for other in ys)
    to_pair = (leaf + 4 - 8 * x_lo, rhs)

    barrier = pltpu.get_barrier_semaphore()
    for device in (to_far, to_mate):
        pl.semaphore_signal(barrier, inc=1, device_id=device, device_id_type=MESH)
    for j in range(3):

        @pl.when(ys[j] > y)
        def _():
            pl.semaphore_signal(barrier, inc=1, device_id=to_ys[j], device_id_type=MESH)

    @pl.when(x_lo == 0)
    def _():
        pl.semaphore_signal(barrier, inc=1, device_id=to_pair, device_id_type=MESH)

    def rows_of(index):
        return pl.ds(pl.multiple_of(index * OWN, OWN), OWN)

    def cols_of(which, k):
        if k < SENT:
            at = which * PANEL + k * PIECE
        else:
            at = KEPT_AT + (which % 2) * KEPT * PIECE + (k - SENT) * PIECE
        return pl.ds(pl.multiple_of(at, PIECE), PIECE)

    def part_of(index):
        return pl.ds(pl.multiple_of(index * PART, PART), PART)

    local = []

    def load(src, dst):
        copy = pltpu.make_async_copy(src, dst, local_sem.at[len(local)])
        copy.start()
        local.append(copy)
        return copy

    def remote(index, src, dst, device):
        return pltpu.make_async_remote_copy(
            src_ref=src, dst_ref=dst, send_sem=send_sem.at[index], recv_sem=recv_sem.at[index],
            device_id=device, device_id_type=MESH,
        )

    def copies(k):
        at = COPIES * k
        c = {}
        if k < SENT:
            c["relay"] = remote(at, x_hbm.at[:, cols_of(cross, k)], relay.at[k], to_mate)
            passed = relay.at[k]
        else:
            passed = xs.at[k, rows_of(mate)]
        c["mate"] = remote(at + 1, x_hbm.at[:, cols_of(mate, k)], xs.at[k, rows_of(rhs)], to_mate)
        c["far"] = remote(at + 2, x_hbm.at[:, cols_of(far, k)], xs.at[k, rows_of(rhs)], to_far)
        c["on"] = remote(at + 3, passed, xs.at[k, rows_of(mate)], to_far)
        c["zero"] = [remote(at + 4 + j, out0.at[k, j], in0.at[k, j], to_ys[j]) for j in range(3)]
        c["one"] = [remote(at + 7 + j, out1.at[k, j], in1.at[k, j], to_ys[j]) for j in range(3)]
        c["two"] = remote(at + 10, out2.at[k], in2.at[k], to_pair)
        c["three"] = [
            remote(at + 11 + j, in2.at[k], sib2.at[k, part_of(y)], to_ys[j]) for j in range(3)
        ]
        if k == EARLY:
            c["half"] = remote(at + 14, out_half, in_half, to_far)
        mine = out.at[:, cols_of(rhs, k)]
        if k < SENT:
            c["rfar"] = remote(at + 14, result.at[k, rows_of(far)], mine, to_far)
            c["back"] = remote(at + 15, result.at[k, rows_of(cross)], back.at[k], to_mate)
            c["ron"] = remote(at + 17, back.at[k], out.at[:, cols_of(mate, k)], to_far)
        c["rmate"] = remote(at + 16, result.at[k, rows_of(mate)], mine, to_mate)
        return c

    every = [copies(k) for k in range(PIECES)]

    pl.semaphore_wait(barrier, 2 + y + x_lo)

    every[0]["far"].start()
    every[0]["relay"].start()
    every[1]["relay"].start()
    every[0]["mate"].start()
    load_noise = load(nugget_hbm, noise)
    load_bases = [
        load(bases_hbm.at[l], bases.at[:, pl.ds(l * RANK, RANK)]) for l in range(LEVELS)
    ]
    every[0]["relay"].wait_recv()
    every[0]["on"].start()
    own_x = [load(x_hbm.at[:, cols_of(rhs, k)], xs.at[k, rows_of(rhs)]) for k in range(PIECES)]
    for k in range(1, PIECES):
        every[k]["mate"].start()
    for j in range(3):

        @pl.when(ys[j] < y)
        def _():
            pl.semaphore_signal(ready, inc=1, device_id=to_ys[j], device_id_type=MESH)

    @pl.when(x_lo == 1)
    def _():
        pl.semaphore_signal(ready, inc=1, device_id=to_pair, device_id_type=MESH)

    count = rows[0:1, :]

    def make_mask(i, carry):
        at = pl.ds(pl.multiple_of(i * BLOCK, BLOCK), BLOCK)
        row = lax.broadcasted_iota(jnp.int32, (BLOCK, PIECE), 0) + i * BLOCK
        mask[at, :] = jnp.where(row < count, 1.0, 0.0).astype(BF16)
        return carry

    lax.fori_loop(0, LEAF // BLOCK, make_mask, 0)

    for copy in load_bases:
        copy.wait()

    def transpose(i, carry):
        at = pl.ds(pl.multiple_of(i * PIECE, PIECE), PIECE)
        for l in range(LEVELS):
            level = pl.ds(l * RANK, RANK)
            bases_t[level, at] = (bases[at, level] * mask[at, :]).T
        return carry

    lax.fori_loop(0, LEAF // PIECE, transpose, 0)

    every[1]["relay"].wait_recv()
    every[1]["far"].start()
    every[1]["on"].start()
    every[2]["far"].start()
    load_near = load(near_hbm, near)
    load_core = load(core_hbm, core)
    load_own = load(x_hbm, own)

    load_noise.wait()
    for i in range(OWN // PIECE):
        at = pl.ds(i * PIECE, PIECE)
        spread_out = jnp.broadcast_to(noise[at].reshape(1, PIECE), (PIECE, PIECE)).T
        alive = mask[pl.ds(pl.multiple_of(rhs * OWN + i * PIECE, PIECE), PIECE), :].astype(F32)
        live[at, :] = alive
        scale[at, :] = spread_out * alive

    def add_noise(cols, value):
        out[:, cols] = (
            value.astype(F32) * live[...] + scale[...] * own[:, cols].astype(F32)
        ).astype(BF16)

    def settle(k, name, which):
        every[k][name].wait_recv()
        cols = cols_of(which, k)
        add_noise(cols, out[:, cols])

    def send_parts(k, part):
        sum2[k] = part
        for j in range(3):
            out1[k, j] = sum2[k, part_of(ys[j])].astype(BF16)
            every[k]["one"][j].start()

    def gather(k):
        c = every[k]
        if k != EARLY:
            own_x[k].wait()
        if k < SENT:
            c["mate"].wait_recv()
        c["far"].wait_recv()
        c["on"].wait_recv()
        if k == EARLY:
            part = jnp.dot(bases_t[: 2 * RANK], xs[k], preferred_element_type=F32)
        else:
            part = jnp.dot(bases_t[...], xs[k], preferred_element_type=F32)
            send_parts(k, part[2 * RANK :])
        middle = part[RANK : 2 * RANK].astype(BF16)
        out0[k, 0] = part[:RANK].astype(BF16)
        out0[k, 1] = middle
        out0[k, 2] = middle
        for copy in c["zero"]:
            copy.start()

    def near_sent(half):
        if half == 0:
            for k in range(SENT):
                xm[:, k * PIECE : (k + 1) * PIECE] = xs[k] * mask[...]
        at = pl.ds(half * CHIP, CHIP)
        total[at, :] = jnp.dot(near[at, :], xm[...], preferred_element_type=F32)

    def near_kept():
        for k in range(KEPT):
            xm[:, k * PIECE : (k + 1) * PIECE] = xs[SENT + k] * mask[...]
        at = pl.ds(pl.multiple_of((rhs // 2) * CHIP, CHIP), CHIP)
        total_kept[...] = jnp.dot(near[at, :], xm[...], preferred_element_type=F32)

    def near_of(k, owner):
        if k < SENT:
            return total[rows_of(owner), k * PIECE : (k + 1) * PIECE]
        at = (k - SENT) * PIECE
        return total_kept[rows_of(owner % 2), at : at + PIECE]

    def quarter(k):
        part = sum2[k, part_of(y)]
        for j in range(3):
            every[k]["one"][j].wait_recv()
            part = part + in1[k, j].astype(F32)
        return part

    def exchange(k):
        out2[k] = quarter(k).astype(BF16)
        every[k]["two"].start()

    def early_parts():
        own_x[EARLY].wait()
        every[EARLY]["mate"].wait_recv()
        at = pl.ds(pl.multiple_of((rhs // 2) * CHIP, CHIP), CHIP)
        send_parts(
            EARLY,
            jnp.dot(bases_t[2 * RANK :, at], xs[EARLY, at], preferred_element_type=F32),
        )

    def early_half():
        part = quarter(EARLY)
        mine_half[...] = part
        out_half[...] = part.astype(BF16)
        every[EARLY]["half"].start()

    def early_exchange():
        every[EARLY]["half"].wait_recv()
        out2[EARLY] = (mine_half[...] + in_half[...].astype(F32)).astype(BF16)
        every[EARLY]["two"].start()

    def spread(k):
        c = every[k]
        c["two"].wait_recv()
        for copy in c["three"]:
            copy.start()
        sib2[k, part_of(y)] = in2[k]

    def finish(k):
        c = every[k]
        for copy in c["zero"] + c["three"]:
            copy.wait_recv()
        sibling = (
            in0[k, 0].astype(F32),
            in0[k, 1].astype(F32) + in0[k, 2].astype(F32),
            sib2[k].astype(F32),
        )
        mapped = jnp.concatenate(
            [
                jnp.dot(
                    core[l, 0], sibling[l], precision=lax.Precision.HIGHEST,
                    preferred_element_type=F32,
                ).astype(BF16)
                for l in range(LEVELS)
            ],
            axis=0,
        )
        owners = ((mate, "rmate"),)
        if k < SENT:
            first = ((far, "rfar"), (cross, "back"))
            owners = (first[::-1] if k else first) + owners
        for owner, name in owners:
            at = rows_of(owner)
            value = near_of(k, owner) + jnp.dot(
                bases[at, :], mapped, preferred_element_type=F32
            )
            result[k, at, :] = value.astype(BF16)
            c[name].start()
        at = rows_of(rhs)
        value = near_of(k, rhs) + jnp.dot(bases[at, :], mapped, preferred_element_type=F32)
        add_noise(cols_of(rhs, k), value.astype(BF16))

    @pl.when(y + x_lo < 4)
    def _():
        pl.semaphore_wait(ready, 4 - y - x_lo)

    early_parts()
    gather(0)
    load_near.wait()
    load_core.wait()
    load_own.wait()
    early_half()
    exchange(0)
    every[2]["mate"].wait_recv()
    every[2]["on"].start()
    every[3]["far"].start()
    gather(1)
    spread(0)
    near_sent(0)
    near_sent(1)
    exchange(1)
    early_exchange()
    every[3]["on"].start()
    gather(2)
    finish(0)
    spread(1)
    exchange(2)
    every[0]["back"].wait_recv()
    every[0]["ron"].start()
    gather(3)
    spread(3)
    finish(1)
    every[1]["back"].wait_recv()
    every[1]["ron"].start()
    spread(2)
    near_kept()
    finish(3)
    settle(0, "rmate", mate)
    settle(1, "rmate", mate)
    settle(0, "rfar", far)
    finish(2)
    settle(0, "ron", cross)
    settle(3, "rmate", mate)
    settle(2, "rmate", mate)
    for k in range(PIECES):
        c = every[k]
        for name in ("relay", "mate", "far", "on", "half", "two", "rfar", "back", "rmate", "ron"):
            if name in c and c[name] is not every[1]["ron"]:
                c[name].wait_send()
        for copy in c["zero"] + c["one"] + c["three"]:
            copy.wait_send()
    settle(1, "rfar", far)
    settle(1, "ron", cross)
    every[1]["ron"].wait_send()


def on_device(*arrays):
    hbm = pl.BlockSpec(memory_space=pltpu.HBM)
    dma = pltpu.SemaphoreType.DMA
    return pl.pallas_call(
        kernel,
        out_shape=pltpu.VMEM((OWN, RHS), BF16),
        in_specs=[hbm] * 4 + [pl.BlockSpec(memory_space=pltpu.VMEM), hbm],
        out_specs=pl.BlockSpec(memory_space=pltpu.VMEM),
        scratch_shapes=[
            pltpu.VMEM((OWN, RHS), BF16),
            pltpu.VMEM((OWN,), F32),
            pltpu.VMEM((OWN, PIECE), F32),
            pltpu.VMEM((OWN, PIECE), F32),
            pltpu.VMEM((PIECES, LEAF, PIECE), BF16),
            pltpu.VMEM((SENT, OWN, PIECE), BF16),
            pltpu.VMEM((LEAF, SENT * PIECE), BF16),
            pltpu.VMEM((LEAF, LEAF), BF16),
            pltpu.VMEM((LEAF, LEVELS * RANK), BF16),
            pltpu.VMEM((LEVELS * RANK, LEAF), BF16),
            pltpu.VMEM((LEVELS, 1, RANK, RANK), F32),
            pltpu.VMEM((LEAF, PIECE), BF16),
            pltpu.VMEM((LEAF, SENT * PIECE), F32),
            pltpu.VMEM((CHIP, KEPT * PIECE), F32),
            pltpu.VMEM((PIECES, LEAF, PIECE), BF16),
            pltpu.VMEM((SENT, OWN, PIECE), BF16),
            pltpu.VMEM((PIECES, 3, RANK, PIECE), BF16),
            pltpu.VMEM((PIECES, 3, RANK, PIECE), BF16),
            pltpu.VMEM((PIECES, 3, PART, PIECE), BF16),
            pltpu.VMEM((PIECES, 3, PART, PIECE), BF16),
            pltpu.VMEM((PIECES, RANK, PIECE), F32),
            pltpu.VMEM((PIECES, PART, PIECE), BF16),
            pltpu.VMEM((PIECES, PART, PIECE), BF16),
            pltpu.VMEM((PIECES, RANK, PIECE), BF16),
            pltpu.VMEM((PART, PIECE), F32),
            pltpu.VMEM((PART, PIECE), BF16),
            pltpu.VMEM((PART, PIECE), BF16),
            dma((12,)),
            dma((COPIES * PIECES,)),
            dma((COPIES * PIECES,)),
            pltpu.SemaphoreType.REGULAR,
        ],
        compiler_params=pltpu.CompilerParams(
            collective_id=0, has_side_effects=True, vmem_limit_bytes=48 << 20
        ),
        cost_estimate=pl.CostEstimate(
            flops=4 * 10**9, bytes_accessed=15 * 10**6, transcendentals=0
        ),
        name="operator",
    )(
        *(pltpu.with_memory_space_constraint(array, pltpu.HBM) for array in arrays[:4]),
        jnp.broadcast_to(arrays[4], (8, PIECE)),
        pltpu.with_memory_space_constraint(arrays[5], pltpu.HBM),
    )


def solution(mesh):
    in_specs = (
        P(("leaf", "rhs"), None),
        P("leaf", None),
        P(None, "leaf", None),
        P(None, "leaf", None, None),
        P("leaf"),
        P(("leaf", "rhs")),
    )
    return jax.shard_map(
        on_device, mesh=mesh, in_specs=in_specs, out_specs=P(("leaf", "rhs"), None), check_vma=False
    )
```
